256 devices in a mesh: ctx: 32 (over z, x), head: 8 (over y, core).
Axes of the slice: x: 4, y: 4, z: 8, core: 2. Of those that a mesh axis runs over, the one named last changes fastest.
Arguments:
- cross_query: bfloat16 [16384, 3072], P('ctx', 'head'), may hold values from -130 to 130
- cross_grad: bfloat16 [16384, 3072], P('ctx', 'head'), may hold values from -6 to 6
- cache_keys: bfloat16 [16384, 1024], P(('ctx', 'head')), may hold values from -6 to 6
- cache_values: bfloat16 [16384, 1024], P(('ctx', 'head')), may hold values from -6 to 6
- retention_query: bfloat16 [16384, 3072], P('ctx', 'head'), may hold values from -3 to 3
- retention_key: bfloat16 [16384, 3072], P('ctx', 'head'), may hold values from -3 to 3
- retention_value: bfloat16 [16384, 3072], P('ctx', 'head'), may hold values from -6 to 6
- retention_grad: bfloat16 [16384, 3072], P('ctx', 'head'), may hold values from -0.59765625 to 0.59765625
- log_decay: float32 [24, 16384], P('head', 'ctx'), may hold values from -2 to 0
- doc_offsets: int32 [87], replicated, may hold values from 0 to 16384, as said below
Outputs:
- cross_query_grad: bfloat16 [16384, 3072], P('ctx', 'head')
- cache_keys_grad: bfloat16 [16384, 1024], P(('ctx', 'head'))
- cache_values_grad: bfloat16 [16384, 1024], P(('ctx', 'head'))
- retention_query_grad: bfloat16 [16384, 3072], P('ctx', 'head')
- retention_key_grad: bfloat16 [16384, 3072], P('ctx', 'head')
- retention_value_grad: bfloat16 [16384, 3072], P('ctx', 'head')
- decay_grad: float32 [24, 16384], P('head', 'ctx')
The draws below stay inside these ranges and needn't reach their ends.
Inputs may be any that keep to these rules, and one draw needn't show every extreme that they name: doc_offsets[0] = 0; the entries never fall; document i holds positions doc_offsets[i] to doc_offsets[i+1] - 1; consecutive entries differ by at most 1536, by exactly 1536 at least once; the entries after the sequence's end equal 16384.
All inputs are finite; a program needn't handle non-finite values.
Results may differ from the reference program's by a relative error of at most 0.003.
The reference program's roundings to bfloat16 on the way count: a program that leaves them out, or rounds other values in their place, can miss the bound.
Values may be sent and summed in bfloat16 or wider, within the bound.
A program may use at most 128 MiB of HBM per device.

```python
import math
import jax
import jax.numpy as jnp
from jax import lax

ATTENDER_NUMBER = 24
KV_HEADS = 8
DH = 128
TOK_DEV = 512
DOC_DEVS = 3
SEQUENCE_LENGTH = 16384
DOC_MAX = 1536
NOFF = 87
N_CTX = 32


def doc_bounds(key):
    stream = jax.random.fold_in(key, 55)
    first, second = jax.random.split(stream)
    doc_count = NOFF - 1
    lengths = jax.random.randint(first, (doc_count,), DOC_MAX // 8, DOC_MAX + 1)
    chosen = jax.random.randint(second, (), 0, SEQUENCE_LENGTH // DOC_MAX)
    lengths = jnp.where(jnp.arange(doc_count) == chosen, DOC_MAX, lengths)
    finishes = jnp.minimum(jnp.cumsum(lengths), SEQUENCE_LENGTH)
    return jnp.concatenate([jnp.zeros((1,), jnp.int32), finishes.astype(jnp.int32)])


def key_table(key):
    stream = jax.random.fold_in(key, 77)
    return jnp.clip(jax.random.normal(stream, (SEQUENCE_LENGTH, KV_HEADS * DH), jnp.float32), -6.0, 6.0)


def draw_doc_offsets(key, part):
    return doc_bounds(key)


def draw_cache_keys(key, part):
    key_rows = key_table(key)
    return key_rows.astype(jnp.bfloat16)


def draw_cross_query(key, part):
    stream = jax.random.fold_in(key, 9)
    queries = jnp.clip(jax.random.normal(stream, (SEQUENCE_LENGTH, ATTENDER_NUMBER * DH), jnp.float32), -6.0, 6.0)
    return queries.astype(jnp.bfloat16)


def draw_log_decay(key, part):
    key = jax.random.fold_in(key, 3)
    concurrent_lanes = jax.random.split(key, 7)
    slow_share = 0.5
    slow_heads = jax.random.bernoulli(concurrent_lanes[0], slow_share, (ATTENDER_NUMBER, 1))
    slow_rate = jnp.exp(jax.random.uniform(concurrent_lanes[1], (ATTENDER_NUMBER, 1), jnp.float32, math.log(0.05), math.log(0.5)))
    slow_rate = slow_rate * math.log(10.0) / SEQUENCE_LENGTH
    fast_rate = jnp.exp(jax.random.uniform(concurrent_lanes[2], (ATTENDER_NUMBER, 1), jnp.float32, math.log(10.0), math.log(17.0)))
    fast_rate = fast_rate / TOK_DEV
    per_iteration_tally = jnp.where(slow_heads, slow_rate, fast_rate)
    ragged_quantity = jnp.exp(jax.random.uniform(concurrent_lanes[3], (ATTENDER_NUMBER, SEQUENCE_LENGTH), jnp.float32, -math.log(2.0), math.log(2.0)))
    processor_rank = jnp.exp(jax.random.uniform(concurrent_lanes[4], (ATTENDER_NUMBER, SEQUENCE_LENGTH // TOK_DEV), jnp.float32, -math.log(2.0), math.log(2.0)))
    processor_rank = jnp.repeat(processor_rank, TOK_DEV, axis=1)
    packet_batches = jax.random.bernoulli(concurrent_lanes[5], 3.0 / SEQUENCE_LENGTH, (ATTENDER_NUMBER, SEQUENCE_LENGTH)).astype(jnp.float32)
    packet_batches = packet_batches * jax.random.uniform(concurrent_lanes[6], (ATTENDER_NUMBER, SEQUENCE_LENGTH), jnp.float32, math.log(1.25), math.log(2.0))
    return (-(per_iteration_tally * ragged_quantity * processor_rank) - packet_batches).astype(jnp.float32)


def block_levels(stream_key, shape, shards, least, top_value):
    level, own = 1.0, jax.random.fold_in(stream_key, 6)
    for axis_at, parts in shards:
        heights = jnp.exp(jax.random.uniform(jax.random.fold_in(own, axis_at), (parts,), jnp.float32, least / len(shards), top_value / len(shards)))
        level = level * jnp.repeat(heights, shape[axis_at] // parts).reshape([-1 if axis == axis_at else 1 for axis in range(len(shape))])
    return level


def gaussian(rng, shape, deviation, reach, shards=(), kind=jnp.bfloat16):
    entries = jax.random.normal(rng, shape, jnp.float32) * deviation
    if len(shards) > 0:
        entries = block_levels(rng, shape, shards, -0.22, 0.18) * entries
    return jnp.clip(entries, min=-reach, max=reach).astype(kind)


def setup_inputs(seed: int = 0) -> dict:
    keys = jax.random.split(jax.random.key(seed), 11)
    cross_query = draw_cross_query(jax.random.fold_in(keys[10], 71), 0)
    cross_grad = gaussian(keys[1], (SEQUENCE_LENGTH, ATTENDER_NUMBER * DH), 1.0, 6.0, ((0, 32), (1, 8)))
    cache_keys = draw_cache_keys(jax.random.fold_in(keys[10], 71), 0)
    cache_values = gaussian(keys[3], (SEQUENCE_LENGTH, KV_HEADS * DH), 1.0, 6.0, ((0, 256),))
    retention_query = gaussian(keys[4], (SEQUENCE_LENGTH, ATTENDER_NUMBER * DH), 0.5, 3.0, ((0, 32), (1, 8)))
    retention_key = gaussian(keys[5], (SEQUENCE_LENGTH, ATTENDER_NUMBER * DH), 0.5, 3.0, ((0, 32), (1, 8)))
    retention_value = gaussian(keys[6], (SEQUENCE_LENGTH, ATTENDER_NUMBER * DH), 1.0, 6.0, ((0, 32), (1, 8)))
    retention_grad = gaussian(keys[7], (SEQUENCE_LENGTH, ATTENDER_NUMBER * DH), 0.1, 0.59765625, ((0, 32), (1, 8)))
    log_decay = draw_log_decay(jax.random.fold_in(keys[10], 71), 0)
    doc_offsets = draw_doc_offsets(jax.random.fold_in(keys[10], 71), 0)
    return {"cross_query": cross_query, "cross_grad": cross_grad, "cache_keys": cache_keys, "cache_values": cache_values, "retention_query": retention_query, "retention_key": retention_key, "retention_value": retention_value, "retention_grad": retention_grad, "log_decay": log_decay, "doc_offsets": doc_offsets}


def doc_index(offsets, positions):
    return jnp.sum((offsets[None, :] <= positions[:, None]).astype(jnp.int32), axis=1) - 1


def barrier_round(values):
    return lax.optimization_barrier(values.astype(jnp.bfloat16)).astype(jnp.float32)


def block_summary(log_block, doc_block, before_doc):
    cum = jnp.cumsum(log_block, axis=1)
    final_doc = doc_block[-1]
    last_w = jnp.where((doc_block == final_doc)[None, :], jnp.exp(cum[:, -1:] - cum), 0.0)
    first_w = jnp.where((doc_block == before_doc)[None, :], jnp.exp(cum), 0.0)
    carried = jnp.where(final_doc == before_doc, jnp.exp(cum[:, -1]), 0.0)
    return cum, last_w, first_w, carried


def cross_part(cross_query, cross_grad, cache_keys, cache_values, doc_ids):
    scaling = DH ** -0.5
    per_group = ATTENDER_NUMBER // KV_HEADS
    window = min((DOC_DEVS + 1) * TOK_DEV, SEQUENCE_LENGTH)
    queries = cross_query.reshape(SEQUENCE_LENGTH, KV_HEADS, per_group, DH).astype(jnp.float32)
    upstream = cross_grad.reshape(SEQUENCE_LENGTH, KV_HEADS, per_group, DH).astype(jnp.float32)
    key_rows = cache_keys.reshape(SEQUENCE_LENGTH, KV_HEADS, DH).astype(jnp.float32)
    value_rows = cache_values.reshape(SEQUENCE_LENGTH, KV_HEADS, DH).astype(jnp.float32)

    def one_block(totals, block_id):
        key_total, value_total = totals
        qstart = (block_id * TOK_DEV).astype(jnp.int32)
        kstart = jnp.clip((block_id - DOC_DEVS) * TOK_DEV, 0, SEQUENCE_LENGTH - window).astype(jnp.int32)
        query_blk = lax.dynamic_slice_in_dim(queries, qstart, TOK_DEV, 0)
        grad_blk = lax.dynamic_slice_in_dim(upstream, qstart, TOK_DEV, 0)
        key_blk = lax.dynamic_slice_in_dim(key_rows, kstart, window, 0)
        value_blk = lax.dynamic_slice_in_dim(value_rows, kstart, window, 0)
        query_pos = qstart + jnp.arange(TOK_DEV, dtype=jnp.int32)
        key_pos = kstart + jnp.arange(window, dtype=jnp.int32)
        query_doc = lax.dynamic_slice_in_dim(doc_ids, qstart, TOK_DEV, 0)
        key_doc = lax.dynamic_slice_in_dim(doc_ids, kstart, window, 0)
        allowed = (query_doc[:, None] == key_doc[None, :]) & (key_pos[None, :] <= query_pos[:, None])
        scores = jnp.einsum("tgad,kgd->gatk", query_blk, key_blk) * scaling
        masked = jnp.where(allowed, scores, -1e30)
        row_top = jnp.max(masked, axis=-1, keepdims=True)
        exponent = jnp.where(allowed, jnp.exp(masked - row_top), 0.0)
        weights = exponent / jnp.sum(exponent, axis=-1, keepdims=True)
        weights_b = barrier_round(weights)
        attended = jnp.einsum("gatk,kgd->tgad", weights_b, value_blk)
        row_dot = jnp.transpose(jnp.sum(grad_blk * attended, axis=-1), (1, 2, 0))[..., None]
        dweights = jnp.einsum("tgad,kgd->gatk", grad_blk, value_blk)
        dscores_b = barrier_round(weights * (dweights - row_dot))
        query_out = (jnp.einsum("gatk,kgd->tgad", dscores_b, key_blk) * scaling).astype(jnp.bfloat16)
        key_part = jnp.einsum("gatk,tgad->kgd", dscores_b, query_blk) * scaling
        value_part = jnp.einsum("gatk,tgad->kgd", weights_b, grad_blk)
        key_total = lax.dynamic_update_slice_in_dim(
            key_total, lax.dynamic_slice_in_dim(key_total, kstart, window, 0) + key_part, kstart, 0)
        value_total = lax.dynamic_update_slice_in_dim(
            value_total, lax.dynamic_slice_in_dim(value_total, kstart, window, 0) + value_part, kstart, 0)
        return (key_total, value_total), query_out

    empty = jnp.zeros((SEQUENCE_LENGTH, KV_HEADS, DH), jnp.float32)
    (key_total, value_total), query_out = lax.scan(one_block, (empty, empty), jnp.arange(N_CTX, dtype=jnp.int32))
    return (query_out.reshape(SEQUENCE_LENGTH, ATTENDER_NUMBER * DH),
            key_total.reshape(SEQUENCE_LENGTH, KV_HEADS * DH).astype(jnp.bfloat16),
            value_total.reshape(SEQUENCE_LENGTH, KV_HEADS * DH).astype(jnp.bfloat16))


def retention_part(retention_query, retention_key, retention_value, retention_grad, log_decay, doc_ids):
    scaling = DH ** -0.5
    query_all = retention_query.reshape(N_CTX, TOK_DEV, ATTENDER_NUMBER, DH).astype(jnp.float32)
    key_all = retention_key.reshape(N_CTX, TOK_DEV, ATTENDER_NUMBER, DH).astype(jnp.float32)
    value_all = retention_value.reshape(N_CTX, TOK_DEV, ATTENDER_NUMBER, DH).astype(jnp.float32)
    grad_all = retention_grad.reshape(N_CTX, TOK_DEV, ATTENDER_NUMBER, DH).astype(jnp.float32)
    log_blocks = jnp.transpose(log_decay.reshape(ATTENDER_NUMBER, N_CTX, TOK_DEV), (1, 0, 2))
    doc_blocks = doc_ids.reshape(N_CTX, TOK_DEV)
    before_docs = jnp.concatenate([jnp.full((1,), -1, jnp.int32), doc_blocks[:-1, -1]])

    def summarize(inputs):
        log_block, doc_block, before_doc, query_blk, key_blk, value_blk, grad_blk = inputs
        cum, last_w, first_w, carried = block_summary(log_block, doc_block, before_doc)
        keys_w = barrier_round(last_w.T[:, :, None] * key_blk)
        queries_w = barrier_round(scaling * first_w.T[:, :, None] * query_blk)
        own_state = jnp.einsum("thd,the->hde", keys_w, value_blk)
        own_grad = jnp.einsum("thd,the->hde", queries_w, grad_blk)
        return carried, own_state, own_grad

    block_inputs = (log_blocks, doc_blocks, before_docs, query_all, key_all, value_all, grad_all)
    carried, own_state, own_grad = lax.map(summarize, block_inputs)

    def forward(state, inputs):
        carry_now, own_now = inputs
        return carry_now[:, None, None] * state + own_now, state

    def backward(later, inputs):
        carry_now, grad_now = inputs
        return grad_now + carry_now[:, None, None] * later, later

    empty = jnp.zeros((ATTENDER_NUMBER, DH, DH), jnp.float32)
    _, states = lax.scan(forward, empty, (carried, own_state))
    _, laters = lax.scan(backward, empty, (carried, own_grad), reverse=True)

    def block_grads(inputs):
        log_block, doc_block, before_doc, query_blk, key_blk, value_blk, grad_blk, state, later = inputs
        cum, last_w, first_w, carried_now = block_summary(log_block, doc_block, before_doc)
        state_b = barrier_round(state)
        later_b = barrier_round(later)
        positions = jnp.arange(TOK_DEV, dtype=jnp.int32)
        same = (doc_block[:, None] == doc_block[None, :]) & (positions[None, :] <= positions[:, None])
        within = jnp.where(same[None], jnp.exp(jnp.minimum(cum[:, :, None] - cum[:, None, :], 0.0)), 0.0)
        grad_dots = jnp.einsum("thd,shd->hts", grad_blk, value_blk)
        query_dots = jnp.einsum("thd,shd->hts", query_blk, key_blk)
        grad_w = barrier_round(scaling * within * grad_dots)
        score_w = barrier_round(scaling * within * query_dots)
        query_f = jnp.einsum("hts,shd->thd", grad_w, key_blk) + (scaling * first_w).T[:, :, None] * jnp.einsum(
            "the,hde->thd", grad_blk, state_b)
        key_f = jnp.einsum("hts,thd->shd", grad_w, query_blk) + last_w.T[:, :, None] * jnp.einsum(
            "she,hde->shd", value_blk, later_b)
        value_f = jnp.einsum("hts,the->she", score_w, grad_blk) + last_w.T[:, :, None] * jnp.einsum(
            "shd,hde->she", key_blk, later_b)
        residue = jnp.sum(query_blk * query_f, axis=-1) - jnp.sum(key_blk * key_f, axis=-1)
        return (query_f.astype(jnp.bfloat16), key_f.astype(jnp.bfloat16), value_f.astype(jnp.bfloat16), residue)

    query_g, key_g, value_g, residue = lax.map(block_grads, block_inputs + (states, laters))
    residue = residue.reshape(SEQUENCE_LENGTH, ATTENDER_NUMBER)
    decay = jnp.flip(jnp.cumsum(jnp.flip(residue, 0), axis=0), 0).T
    return (query_g.reshape(SEQUENCE_LENGTH, ATTENDER_NUMBER * DH), key_g.reshape(SEQUENCE_LENGTH, ATTENDER_NUMBER * DH),
            value_g.reshape(SEQUENCE_LENGTH, ATTENDER_NUMBER * DH), decay)


def reference(cross_query, cross_grad, cache_keys, cache_values, retention_query, retention_key,
              retention_value, retention_grad, log_decay, doc_offsets):
    doc_ids = doc_index(doc_offsets, jnp.arange(SEQUENCE_LENGTH, dtype=jnp.int32))
    query_grad, keys_grad, values_grad = cross_part(cross_query, cross_grad, cache_keys, cache_values, doc_ids)
    rquery_grad, rkey_grad, rvalue_grad, decay = retention_part(
        retention_query, retention_key, retention_value, retention_grad, log_decay, doc_ids)
    return (query_grad, keys_grad, values_grad, rquery_grad, rkey_grad, rvalue_grad, decay)
```

```python
import jax
import jax.numpy as jnp
from jax import lax
from jax.sharding import PartitionSpec as P

ATTENDER_NUMBER = 24
KV_HEADS = 8
DH = 128
DOC_DEVS = 3


def from_behind(block, axis, distance):
    devices = range(lax.axis_size(axis))
    route = [(i - distance, i) for i in devices if i - distance in devices]
    return lax.ppermute(block, axis, route)


def doc_index(offsets, positions):
    return jnp.sum((offsets[None, :] <= positions[:, None]).astype(jnp.int32), axis=1) - 1


def block_summary(log_block, doc_block, before_doc):
    cum = jnp.cumsum(log_block, axis=1)
    final_doc = doc_block[-1]
    last_w = jnp.where((doc_block == final_doc)[None, :], jnp.exp(cum[:, -1:] - cum), 0.0)
    first_w = jnp.where((doc_block == before_doc)[None, :], jnp.exp(cum), 0.0)
    carried = jnp.where(final_doc == before_doc, jnp.exp(cum[:, -1]), 0.0)
    return (cum, last_w, first_w, carried)


def on_device(
    cross_query,
    cross_grad,
    cache_keys,
    cache_values,
    retention_query,
    retention_key,
    retention_value,
    retention_grad,
    log_decay,
    doc_offsets,
):
    scaling = DH ** (-0.5)
    per_group = ATTENDER_NUMBER // KV_HEADS
    local_rows = cross_query.shape[0]
    my_rank = lax.axis_index("ctx")
    ctx_count = lax.axis_size("ctx")
    query_pos = my_rank * local_rows + jnp.arange(local_rows, dtype=jnp.int32)
    query_doc = doc_index(doc_offsets, query_pos)
    key_rows, value_rows = (
        lax.all_to_all(cache_keys, "head", split_axis=1, concat_axis=0, tiled=True),
        lax.all_to_all(cache_values, "head", split_axis=1, concat_axis=0, tiled=True),
    )
    kv_local = key_rows.shape[1] // DH
    queries = cross_query.reshape(local_rows, kv_local, per_group, DH)
    upstream = cross_grad.reshape(local_rows, kv_local, per_group, DH)
    arrived = [(key_rows, value_rows)]
    for distance in range(1, DOC_DEVS + 1):
        arrived.append(from_behind((key_rows, value_rows), "ctx", distance))
    prepared = []
    for distance in range(DOC_DEVS + 1):
        key_pos = (my_rank - distance) * local_rows + jnp.arange(local_rows, dtype=jnp.int32)
        key_doc = doc_index(doc_offsets, key_pos)
        allowed = (query_doc[:, None] == key_doc[None, :]) & (
            key_pos[None, :] <= query_pos[:, None]
        )
        live = key_doc[-1] >= query_doc[0]
        prepared.append(
            (
                arrived[distance][0].reshape(local_rows, kv_local, DH),
                arrived[distance][1].reshape(local_rows, kv_local, DH),
                allowed,
                live,
            )
        )

    def scores_of(item):
        return (
            jnp.einsum("tgad,kgd->gatk", queries, item[0], preferred_element_type=jnp.float32)
            * scaling
        )

    stats = (
        jnp.full((kv_local, per_group, local_rows), -1e30, jnp.float32),
        jnp.zeros((kv_local, per_group, local_rows), jnp.float32),
    )
    for item in prepared:
        stats_row_top, stats_row_sum = stats
        stats_masked = jnp.where(item[2], scores_of(item), -1e30)
        new_top = jnp.maximum(stats_row_top, jnp.max(stats_masked, axis=-1))
        terms = jnp.where(item[2], jnp.exp(stats_masked - new_top[..., None]), 0.0)
        stats = (
            new_top,
            stats_row_sum * jnp.exp(stats_row_top - new_top) + jnp.sum(terms, axis=-1),
        )
    row_top, row_sum = stats

    def weights_of(item):
        masked = jnp.where(item[2], scores_of(item), -1e30)
        exponent = jnp.where(item[2], jnp.exp(masked - row_top[..., None]), 0.0)
        return exponent / row_sum[..., None]

    attended = jnp.zeros((local_rows, kv_local, per_group, DH), jnp.float32)
    for item in prepared:
        output_weights_b = weights_of(item).astype(jnp.bfloat16)
        attended = attended + jnp.einsum(
            "gatk,kgd->tgad", output_weights_b, item[1], preferred_element_type=jnp.float32
        )
    row_dot = jnp.transpose(jnp.sum(upstream.astype(jnp.float32) * attended, axis=-1), (1, 2, 0))[
        ..., None
    ]
    zero_rows = jnp.zeros((local_rows, kv_local, DH), jnp.float32)
    query_total = jnp.zeros((local_rows, kv_local, per_group, DH), jnp.float32)
    key_sum = zero_rows
    value_sum = zero_rows
    for distance in range(DOC_DEVS + 1):
        grad_item = prepared[distance]
        grad_query_total = query_total
        weights = weights_of(grad_item)
        weights_b = weights.astype(jnp.bfloat16)
        dweights = jnp.einsum(
            "tgad,kgd->gatk", upstream, grad_item[1], preferred_element_type=jnp.float32
        )
        dscores_b = (weights * (dweights - row_dot)).astype(jnp.bfloat16)
        grad_query_total = grad_query_total + jnp.einsum(
            "gatk,kgd->tgad", dscores_b, grad_item[0], preferred_element_type=jnp.float32
        )
        key_part = (
            jnp.einsum("gatk,tgad->kgd", dscores_b, queries, preferred_element_type=jnp.float32)
            * scaling
        )
        value_part = jnp.einsum(
            "gatk,tgad->kgd", weights_b, upstream, preferred_element_type=jnp.float32
        )
        query_total, key_part, value_part = (grad_query_total, key_part, value_part)
        if distance == 0:
            key_sum = key_part
            value_sum = value_part
        else:
            key_back, value_back = from_behind((key_part, value_part), "ctx", -distance)
            key_sum = key_sum + key_back
            value_sum = value_sum + value_back
    cross_query_grad = (
        (query_total * scaling).astype(jnp.bfloat16).reshape(local_rows, kv_local * per_group * DH)
    )
    key_flat = key_sum.reshape(local_rows, kv_local * DH).astype(jnp.bfloat16)
    value_flat = value_sum.reshape(local_rows, kv_local * DH).astype(jnp.bfloat16)
    cache_keys_grad, cache_values_grad = (
        lax.all_to_all(key_flat, "head", split_axis=0, concat_axis=1, tiled=True),
        lax.all_to_all(value_flat, "head", split_axis=0, concat_axis=1, tiled=True),
    )
    heads_local = retention_query.shape[1] // DH
    query_rows = retention_query.reshape(local_rows, heads_local, DH)
    retained_keys = retention_key.reshape(local_rows, heads_local, DH)
    retained_values = retention_value.reshape(local_rows, heads_local, DH)
    retained_grad = retention_grad.reshape(local_rows, heads_local, DH)
    before_doc = doc_index(doc_offsets, jnp.reshape(my_rank * local_rows - 1, (1,)))[0]
    cum, last_w, first_w, carried = block_summary(log_decay, query_doc, before_doc)
    keys_w = (last_w.T[:, :, None] * retained_keys.astype(jnp.float32)).astype(jnp.bfloat16)
    queries_w = (scaling * first_w.T[:, :, None] * query_rows.astype(jnp.float32)).astype(
        jnp.bfloat16
    )
    own_state = jnp.einsum(
        "thd,the->hde", keys_w, retained_values, preferred_element_type=jnp.float32
    )
    own_grad = jnp.einsum(
        "thd,the->hde", queries_w, retained_grad, preferred_element_type=jnp.float32
    )
    zeros_state = jnp.zeros((heads_local, DH, DH), jnp.float32)

    carried_state = jnp.concatenate(
        [own_state.reshape(heads_local, DH * DH), jnp.broadcast_to(carried[:, None], (heads_local, DH))],
        axis=1,
    )
    carried_grad = jnp.concatenate(
        [own_grad.reshape(heads_local, DH * DH), jnp.broadcast_to(carried[:, None], (heads_local, DH))],
        axis=1,
    )
    state = zeros_state
    later_grad = zeros_state
    forward_scale = jnp.ones((heads_local, 1, 1), jnp.float32)
    backward_scale = jnp.ones((heads_local, 1, 1), jnp.float32)
    for distance in range(1, DOC_DEVS + 1):
        before = from_behind(carried_state, "ctx", distance)
        after = from_behind(carried_grad, "ctx", -distance)
        state = state + forward_scale * before[:, : DH * DH].reshape(heads_local, DH, DH)
        later_grad = later_grad + backward_scale * after[:, : DH * DH].reshape(heads_local, DH, DH)
        forward_scale = forward_scale * before[:, DH * DH :][:, :1, None]
        backward_scale = backward_scale * after[:, DH * DH :][:, :1, None]
    state_b = state.astype(jnp.bfloat16)
    later_b = later_grad.astype(jnp.bfloat16)
    positions = jnp.arange(local_rows, dtype=jnp.int32)
    same = (query_doc[:, None] == query_doc[None, :]) & (positions[None, :] <= positions[:, None])
    within = jnp.where(
        same[None], jnp.exp(jnp.minimum(cum[:, :, None] - cum[:, None, :], 0.0)), 0.0
    )
    grad_dots = jnp.einsum(
        "thd,shd->hts", retained_grad, retained_values, preferred_element_type=jnp.float32
    )
    query_dots = jnp.einsum(
        "thd,shd->hts", query_rows, retained_keys, preferred_element_type=jnp.float32
    )
    grad_w = (scaling * within * grad_dots).astype(jnp.bfloat16)
    score_w = (scaling * within * query_dots).astype(jnp.bfloat16)
    query_f = jnp.einsum(
        "hts,shd->thd", grad_w, retained_keys, preferred_element_type=jnp.float32
    ) + (scaling * first_w).T[:, :, None] * jnp.einsum(
        "the,hde->thd", retained_grad, state_b, preferred_element_type=jnp.float32
    )
    key_f = jnp.einsum(
        "hts,thd->shd", grad_w, query_rows, preferred_element_type=jnp.float32
    ) + last_w.T[:, :, None] * jnp.einsum(
        "she,hde->shd", retained_values, later_b, preferred_element_type=jnp.float32
    )
    value_f = jnp.einsum(
        "hts,the->she", score_w, retained_grad, preferred_element_type=jnp.float32
    ) + last_w.T[:, :, None] * jnp.einsum(
        "shd,hde->she", retained_keys, later_b, preferred_element_type=jnp.float32
    )
    residue = jnp.sum(query_rows.astype(jnp.float32) * query_f, axis=-1) - jnp.sum(
        retained_keys.astype(jnp.float32) * key_f, axis=-1
    )
    residue = residue.T
    suffix = jnp.flip(jnp.cumsum(jnp.flip(residue, 1), axis=1), 1)
    totals = jnp.broadcast_to(jnp.pad(suffix[:, 0], (0, DH - heads_local))[None, :], (ctx_count, DH))
    totals = lax.all_to_all(totals, "ctx", split_axis=0, concat_axis=0, tiled=True)
    after_me = jnp.arange(ctx_count)[:, None] > my_rank
    tail = jnp.sum(jnp.where(after_me, totals, 0.0), axis=0)[:heads_local]
    decay_grad = suffix + tail[:, None]
    return (
        cross_query_grad,
        cache_keys_grad,
        cache_values_grad,
        query_f.astype(jnp.bfloat16).reshape(local_rows, heads_local * DH),
        key_f.astype(jnp.bfloat16).reshape(local_rows, heads_local * DH),
        value_f.astype(jnp.bfloat16).reshape(local_rows, heads_local * DH),
        decay_grad,
    )


def solution(mesh):
    return jax.shard_map(
        on_device,
        mesh=mesh,
        in_specs=(
            P("ctx", "head"),
            P("ctx", "head"),
            P(("ctx", "head"), None),
            P(("ctx", "head"), None),
            P("ctx", "head"),
            P("ctx", "head"),
            P("ctx", "head"),
            P("ctx", "head"),
            P("head", "ctx"),
            P(),
        ),
        out_specs=(
            P("ctx", "head"),
            P(("ctx", "head"), None),
            P(("ctx", "head"), None),
            P("ctx", "head"),
            P("ctx", "head"),
            P("ctx", "head"),
            P("head", "ctx"),
        ),
        check_vma=False,
    )
```

```python
import jax
import jax.numpy as jnp
from jax import lax
from jax.experimental import pallas as pl
from jax.experimental.pallas import tpu as pltpu
from jax.sharding import PartitionSpec as P

ATTENDER_NUMBER = 24
KV_HEADS = 8
DH = 128
PER_GROUP = ATTENDER_NUMBER // KV_HEADS
ROWS = 512
TILE = 256
TILES = ROWS // TILE
X_RING = 4
SCALING = DH ** (-0.5)
EXPONENT_SCALE = SCALING * 1.4426950408889634
MESH = pl.DeviceIdType.MESH
BF16 = jnp.bfloat16
F32 = jnp.float32
STATE_ROWS = PER_GROUP * DH + 8


def matmul(a, b):
    return lax.dot_general(a, b, (((1,), (0,)), ((), ())), preferred_element_type=F32)


def matmul_nt(a, b):
    return lax.dot_general(a, b, (((1,), (1,)), ((), ())), preferred_element_type=F32)


def matmul_tn(a, b):
    return lax.dot_general(a, b, (((0,), (0,)), ((), ())), preferred_element_type=F32)


def exact_pieces(x):
    high = x.astype(BF16)
    rest = x - high.astype(F32)
    middle = rest.astype(BF16)
    low = (rest - middle.astype(F32)).astype(BF16)
    return jnp.concatenate([high, middle, low], axis=0)


def triangle_sum(x, triangle):
    parts = matmul(exact_pieces(x), triangle)
    return parts[0:16] + parts[16:32] + parts[32:48]


def body(
    n_ctx, n_head,
    cq, cg, ck, cv, rq, rk, rv, rg, ld, offs,
    gq, gk, gv, oq, ok, ov, dg,
    kvs, kvb, own_f, own_b, got_f, got_b, part, half, back, home, final, landed, tot_x, tot_z,
    qs, os, kt, score, dprob, prob_t, dscore_t,
    start_row, cum_row, cum_col, last_w, first_w, qf, kf, vf, pad16,
    head_s, head_r, kv_s, kv_r, st_s, st_r, gr_s, gr_r, fin_s, fin_r, tx_s, tx_r, tz_s, tz_r,
):
    c = lax.axis_index("ctx")
    g = lax.axis_index("head")
    z_ring = n_ctx // X_RING
    slot_rows = ROWS // n_head

    def ctx_at(offset):
        return lax.rem(c + (offset + n_ctx), n_ctx)

    def head_at(offset):
        return lax.rem(g + offset, n_head)

    x = lax.rem(c, X_RING)
    z = c // X_RING

    def x_peer(offset):
        return z * X_RING + lax.rem(x + offset, X_RING)

    def z_peer(offset):
        return lax.rem(z + offset, z_ring) * X_RING + x

    def send(src, dst, send_sem, recv_sem, device):
        return pltpu.make_async_remote_copy(
            src_ref=src, dst_ref=dst, send_sem=send_sem, recv_sem=recv_sem,
            device_id=device, device_id_type=MESH,
        )

    partners = [(c, head_at(k)) for k in range(1, n_head)]
    partners += [(ctx_at(k), g) for k in (1, -1, 3, -3)]
    partners += [(x_peer(k), g) for k in range(1, X_RING)]
    partners += [(z_peer(k), g) for k in range(1, z_ring)]
    barrier = pltpu.get_barrier_semaphore()
    for device in partners:
        pl.semaphore_signal(barrier, inc=1, device_id=device, device_id_type=MESH)

    kvs[0] = ck[...]
    kvs[1] = cv[...]
    base = (c * ROWS).astype(F32)
    offsets = offs[...].astype(F32)
    pos_col = lax.broadcasted_iota(jnp.int32, (ROWS, 1), 0).astype(F32)
    begun = jnp.where(offsets <= pos_col + base, offsets, 0.0)
    start_col = jnp.max(begun, axis=1, keepdims=True) - base
    start_row[...] = jnp.broadcast_to(start_col, (ROWS, DH)).T[0:8]
    start_last = start_col[ROWS - 1 : ROWS, :]
    row_at = lax.broadcasted_iota(jnp.int32, (ROWS, ROWS), 0)
    col_at = lax.broadcasted_iota(jnp.int32, (ROWS, ROWS), 1)

    pl.semaphore_wait(barrier, len(partners))

    head_copies = []
    for k in range(1, n_head):
        to = head_at(k)
        copy = send(
            kvs.at[:, :, pl.ds(pl.multiple_of(to * DH, DH), DH)],
            kvb.at[0, :, pl.ds(pl.multiple_of(g * slot_rows, slot_rows), slot_rows), :],
            head_s.at[k], head_r.at[k], (c, to),
        )
        copy.start()
        head_copies.append(copy)
    kvb[0, :, pl.ds(pl.multiple_of(g * slot_rows, slot_rows), slot_rows), :] = kvs[
        :, :, pl.ds(pl.multiple_of(g * DH, DH), DH)
    ]

    pad16[...] = jnp.zeros_like(pad16)
    pad16[0:PER_GROUP, :] = ld[...]
    cum = triangle_sum(pad16[...], (row_at <= col_at).astype(F32).astype(BF16))
    cum_row[...] = cum
    cum_t = jnp.concatenate([cum, jnp.zeros((DH - 16, ROWS), F32)], axis=0).T
    carry_rows = []
    for h in range(PER_GROUP):
        lanes = slice(h * DH, (h + 1) * DH)
        col = cum_t[:, h : h + 1]
        final_cum = col[ROWS - 1 : ROWS, :]
        last = jnp.where(pos_col >= start_last, jnp.exp(final_cum - col), 0.0)
        first = jnp.where(start_col < 0.0, jnp.exp(col), 0.0) * SCALING
        cum_col[h] = jnp.broadcast_to(col, (ROWS, DH))
        last = jnp.broadcast_to(last, (ROWS, DH))
        first = jnp.broadcast_to(first, (ROWS, DH))
        last_w[h] = last
        first_w[h] = first
        keys_w = (last * rk[:, lanes].astype(F32)).astype(BF16)
        queries_w = (first * rq[:, lanes].astype(F32)).astype(BF16)
        own_f[h * DH : (h + 1) * DH, :] = matmul_tn(keys_w, rv[:, lanes])
        own_b[h * DH : (h + 1) * DH, :] = matmul_tn(queries_w, rg[:, lanes])
        carry = jnp.where(start_last < 0.0, jnp.exp(final_cum), 0.0)
        carry_rows.append(jnp.broadcast_to(carry, (8, DH)))
    which = lax.broadcasted_iota(jnp.int32, (8, DH), 0)
    carries = jnp.zeros((8, DH), F32)
    for h in range(PER_GROUP):
        carries = jnp.where(which == h, carry_rows[h], carries)
    own_f[PER_GROUP * DH :, :] = carries
    own_b[PER_GROUP * DH :, :] = carries

    for i in range(TILES):
        for h in range(PER_GROUP):
            at = (i * PER_GROUP + h) * TILE
            qs[at : at + TILE, :] = cq[i * TILE : (i + 1) * TILE, h * DH : (h + 1) * DH]
            os[at : at + TILE, :] = cg[i * TILE : (i + 1) * TILE, h * DH : (h + 1) * DH]

    for copy in head_copies:
        copy.wait_recv()
    kv_copies = [
        send(kvb.at[0], kvb.at[1], kv_s.at[0], kv_r.at[0], (ctx_at(1), g)),
        send(kvb.at[0], kvb.at[3], kv_s.at[1], kv_r.at[1], (ctx_at(3), g)),
        send(kvb.at[1, 0], kvb.at[2, 0], kv_s.at[2], kv_r.at[2], (ctx_at(1), g)),
        send(kvb.at[3, 1], kvb.at[2, 1], kv_s.at[3], kv_r.at[3], (ctx_at(-1), g)),
    ]
    state_copies = [
        send(own_f, got_f.at[0], st_s.at[0], st_r.at[0], (ctx_at(1), g)),
        send(own_b, got_b.at[0], st_s.at[1], st_r.at[1], (ctx_at(-1), g)),
        send(own_f, got_f.at[2], st_s.at[2], st_r.at[2], (ctx_at(3), g)),
        send(own_b, got_b.at[2], st_s.at[3], st_r.at[3], (ctx_at(-3), g)),
        send(got_f.at[0], got_f.at[1], st_s.at[4], st_r.at[4], (ctx_at(1), g)),
        send(got_b.at[0], got_b.at[1], st_s.at[5], st_r.at[5], (ctx_at(-1), g)),
    ]
    kv_copies[0].start()
    kv_copies[1].start()

    tile_row = lax.broadcasted_iota(jnp.int32, (TILE, TILE), 0)
    tile_col = lax.broadcasted_iota(jnp.int32, (TILE, TILE), 1)
    tile_pos = tile_row.astype(F32)
    causal = tile_row <= tile_col

    def retention_head(h, nothing):
        lanes = pl.ds(pl.multiple_of(h * DH, DH), DH)
        for ti in range(TILES):
            t = slice(ti * TILE, (ti + 1) * TILE)
            rq_t = rq[t, lanes]
            rg_t = rg[t, lanes]
            cum_t_row = cum_row[pl.ds(h, 1), t]
            query_t = jnp.zeros((DH, TILE), F32)
            for si in range(ti + 1):
                s = slice(si * TILE, (si + 1) * TILE)
                rk_s = rk[s, lanes]
                allowed = tile_pos >= start_row[0:1, t] - float(si * TILE)
                if si == ti:
                    allowed = allowed & causal
                gap = jnp.minimum(cum_t_row - cum_col[h, s, 0:1], 0.0)
                within = jnp.where(allowed, jnp.exp(gap) * SCALING, 0.0)
                grad_w = (within * matmul_nt(rv[s, lanes], rg_t)).astype(BF16)
                score_w = (within * matmul_nt(rk_s, rq_t)).astype(BF16)
                query_t = query_t + matmul_tn(rk_s, grad_w)
                key_term = matmul(grad_w, rq_t)
                value_term = matmul(score_w, rg_t)
                if si == ti:
                    kf[h, s, :] = key_term
                    vf[h, s, :] = value_term
                else:
                    kf[h, s, :] = kf[h, s, :] + key_term
                    vf[h, s, :] = vf[h, s, :] + value_term
            qf[h, t, :] = query_t.T

        @pl.when(h == 1)
        def _():
            kv_copies[0].wait_recv()
            kv_copies[2].start()
            kv_copies[1].wait_recv()
            kv_copies[3].start()
            for copy in state_copies[:4]:
                copy.start()

        return nothing

    lax.fori_loop(0, PER_GROUP, retention_head, 0)

    kv_copies[2].wait_recv()
    kv_copies[3].wait_recv()
    for d in range(4):
        kt[d] = kvb[d, 0].astype(F32).T.astype(BF16)

    def attention_head(h, nothing):
        for i in range(TILES):
            cols = pl.ds(pl.multiple_of(i * (PER_GROUP * TILE) + h * TILE, TILE), TILE)
            query = qs[cols, :]
            upstream = os[cols, :]
            start_t = start_row[0:1, i * TILE : (i + 1) * TILE]
            pieces = [(0, j) for j in range(i + 1)]
            pieces += [(d, j) for d in (1, 2) for j in range(TILES)]
            pieces += [(3, j) for j in range(i, TILES)]
            top = jnp.full((1, TILE), -1e30, F32)
            for n, (d, j) in enumerate(pieces):
                s = slice(j * TILE, (j + 1) * TILE)
                raw = matmul_nt(kvb[d, 0, s, :], query)
                allowed = tile_pos >= start_t + float(d * ROWS - j * TILE)
                if d == 0 and j == i:
                    allowed = allowed & causal
                raw = jnp.where(allowed, raw, -1e30)
                score[n * TILE : (n + 1) * TILE, :] = raw
                top = jnp.maximum(top, jnp.max(raw, axis=0, keepdims=True))
            total = jnp.zeros((1, TILE), F32)
            for n in range(len(pieces)):
                at = slice(n * TILE, (n + 1) * TILE)
                term = jnp.exp2((score[at, :] - top) * EXPONENT_SCALE)
                score[at, :] = term
                total = total + jnp.sum(term, axis=0, keepdims=True)
            inverse = 1.0 / total
            row_dot = jnp.zeros((1, TILE), F32)
            for n, (d, j) in enumerate(pieces):
                s = slice(j * TILE, (j + 1) * TILE)
                at = slice(n * TILE, (n + 1) * TILE)
                weights = score[at, :] * inverse
                weights_b = weights.astype(BF16)
                dweights = matmul_nt(kvb[d, 1, s, :], upstream)
                score[at, :] = weights
                dprob[at, :] = dweights
                prob_t[d, s, cols] = weights_b
                row_dot = row_dot + jnp.sum(weights_b.astype(F32) * dweights, axis=0, keepdims=True)
            query_t = jnp.zeros((DH, TILE), F32)
            for n, (d, j) in enumerate(pieces):
                s = slice(j * TILE, (j + 1) * TILE)
                at = slice(n * TILE, (n + 1) * TILE)
                dscores_b = (score[at, :] * (dprob[at, :] - row_dot)).astype(BF16)
                dscore_t[d, s, cols] = dscores_b
                query_t = query_t + matmul(kt[d, :, s], dscores_b)
            gq[i * TILE : (i + 1) * TILE, pl.ds(pl.multiple_of(h * DH, DH), DH)] = (
                query_t.T * SCALING
            ).astype(BF16)

        @pl.when(h == 0)
        def _():
            state_copies[0].wait_recv()
            state_copies[4].start()
            state_copies[1].wait_recv()
            state_copies[5].start()

        return nothing

    lax.fori_loop(0, PER_GROUP, attention_head, 0)

    width = PER_GROUP * TILE

    def partial_grads(d, j):
        s = slice(j * TILE, (j + 1) * TILE)
        cols = slice(0, TILES * width)
        if d == 0:
            cols = slice(j * width, TILES * width)
        if d == 3:
            cols = slice(0, (j + 1) * width)
        keys = matmul(dscore_t[d, s, cols], qs[cols, :]) * SCALING
        values = matmul(prob_t[d, s, cols], os[cols, :])
        return keys, values

    grad_copies = [
        send(part.at[1, 0], half.at[0], gr_s.at[0], gr_r.at[0], (ctx_at(-1), g)),
        send(part.at[1, 1], half.at[1], gr_s.at[1], gr_r.at[1], (ctx_at(1), g)),
        send(part.at[2], back.at[1], gr_s.at[2], gr_r.at[2], (ctx_at(-3), g)),
        send(part.at[0], back.at[0], gr_s.at[3], gr_r.at[3], (ctx_at(-1), g)),
    ]
    tiles = [slice(j * TILE, (j + 1) * TILE) for j in range(TILES)]
    for j in range(TILES):
        keys, values = partial_grads(2, j)
        part[1, 0, tiles[j], :] = keys.astype(BF16)
        part[1, 1, tiles[j], :] = values.astype(BF16)
    grad_copies[0].start()
    grad_copies[1].start()
    third = [partial_grads(3, j) for j in range(TILES)]
    for j in range(TILES):
        part[2, 0, tiles[j], :] = third[j][0].astype(BF16)
        home[1, tiles[j], :] = third[j][1]
    grad_copies[1].wait_recv()
    part[2, 1] = (home[1] + half[1].astype(F32)).astype(BF16)
    grad_copies[2].start()
    for j in range(TILES):
        keys, values = partial_grads(1, j)
        home[0, tiles[j], :] = keys
        part[0, 1, tiles[j], :] = values.astype(BF16)
    grad_copies[0].wait_recv()
    part[0, 0] = (home[0] + half[0].astype(F32)).astype(BF16)
    grad_copies[3].start()
    for j in range(TILES):
        keys, values = partial_grads(0, j)
        home[0, tiles[j], :] = keys
        home[1, tiles[j], :] = values

    for copy in state_copies[2:]:
        copy.wait_recv()
    sums = jnp.zeros((ROWS, DH), F32)
    lane_at = lax.broadcasted_iota(jnp.int32, (ROWS, DH), 1)
    for h in range(PER_GROUP):
        lanes = slice(h * DH, (h + 1) * DH)
        block = slice(h * DH, (h + 1) * DH)
        carry_at = slice(PER_GROUP * DH + h, PER_GROUP * DH + h + 1)

        def chained(got):
            inner = got[1, block, :] + got[1, carry_at, :] * got[2, block, :]
            return (got[0, block, :] + got[0, carry_at, :] * inner).astype(BF16)

        state_b = jnp.where(c > 0, chained(got_f), jnp.zeros((DH, DH), BF16))
        later_b = jnp.where(c < n_ctx - 1, chained(got_b), jnp.zeros((DH, DH), BF16))
        last = last_w[h]
        query_f = qf[h] + first_w[h] * matmul_nt(rg[:, lanes], state_b)
        key_f = kf[h] + last * matmul_nt(rv[:, lanes], later_b)
        value_f = vf[h] + last * matmul(rk[:, lanes], later_b)
        oq[:, lanes] = query_f.astype(BF16)
        ok[:, lanes] = key_f.astype(BF16)
        ov[:, lanes] = value_f.astype(BF16)
        residue = jnp.sum(rq[:, lanes].astype(F32) * query_f, axis=1, keepdims=True) - jnp.sum(
            rk[:, lanes].astype(F32) * key_f, axis=1, keepdims=True
        )
        sums = jnp.where(lane_at == h, residue, sums)
    suffix = triangle_sum(sums.T[0:16], (row_at >= col_at).astype(F32).astype(BF16))
    cum_row[...] = suffix
    tot_x[0] = jnp.broadcast_to(suffix[0:8, 0:1], (8, DH))
    x_copies = [
        send(tot_x.at[0], tot_x.at[k], tx_s.at[k], tx_r.at[k], (x_peer(k), g))
        for k in range(1, X_RING)
    ]
    for copy in x_copies:
        copy.start()

    grad_copies[2].wait_recv()
    grad_copies[3].wait_recv()
    for m in range(2):
        total = home[m] + back[0, m].astype(F32) + back[1, m].astype(F32)
        final[m] = total.astype(BF16)
    final_copies = []
    for k in range(1, n_head):
        to = head_at(k)
        copy = send(
            final.at[:, pl.ds(pl.multiple_of(to * slot_rows, slot_rows), slot_rows), :],
            landed.at[:, :, pl.ds(pl.multiple_of(g * DH, DH), DH)],
            fin_s.at[k], fin_r.at[k], (c, to),
        )
        copy.start()
        final_copies.append(copy)
    landed[:, :, pl.ds(pl.multiple_of(g * DH, DH), DH)] = final[
        :, pl.ds(pl.multiple_of(g * slot_rows, slot_rows), slot_rows), :
    ]

    for copy in x_copies:
        copy.wait_recv()
    row_total = tot_x[0]
    tail = jnp.zeros((8, DH), F32)
    for k in range(1, X_RING):
        row_total = row_total + tot_x[k]
        tail = tail + jnp.where(lax.rem(x - k + X_RING, X_RING) > x, tot_x[k], 0.0)
    tot_z[0] = row_total
    z_copies = [
        send(tot_z.at[0], tot_z.at[k], tz_s.at[k], tz_r.at[k], (z_peer(k), g))
        for k in range(1, z_ring)
    ]
    for copy in z_copies:
        copy.start()
    for copy in z_copies:
        copy.wait_recv()
    for k in range(1, z_ring):
        tail = tail + jnp.where(lax.rem(z - k + z_ring, z_ring) > z, tot_z[k], 0.0)
    dg[...] = (cum_row[0:8, :] + tail[:, 0:1])[0:PER_GROUP]

    for copy in final_copies:
        copy.wait_recv()
    gk[...] = landed[0]
    gv[...] = landed[1]
    for copy in (
        head_copies + kv_copies + state_copies + grad_copies + final_copies + x_copies + z_copies
    ):
        copy.wait_send()


def on_device(
    cross_query, cross_grad, cache_keys, cache_values, retention_query, retention_key,
    retention_value, retention_grad, log_decay, doc_offsets,
):
    n_ctx = lax.axis_size("ctx")
    n_head = lax.axis_size("head")
    wide = jax.ShapeDtypeStruct(cross_query.shape, BF16)
    cache = jax.ShapeDtypeStruct(cache_keys.shape, BF16)
    vmem = pl.BlockSpec(memory_space=pltpu.VMEM)
    slot_rows, all_heads = cache_keys.shape
    dma = pltpu.SemaphoreType.DMA
    heads_wide = pltpu.VMEM((PER_GROUP, ROWS, DH), F32)
    return pl.pallas_call(
        lambda *refs: body(n_ctx, n_head, *refs),
        out_shape=(
            wide, cache, cache, wide, wide, wide, jax.ShapeDtypeStruct(log_decay.shape, F32),
        ),
        in_specs=[vmem] * 10,
        out_specs=(vmem,) * 7,
        scratch_shapes=[
            pltpu.VMEM((2, slot_rows, all_heads), BF16),
            pltpu.VMEM((4, 2, ROWS, DH), BF16),
            pltpu.VMEM((STATE_ROWS, DH), F32),
            pltpu.VMEM((STATE_ROWS, DH), F32),
            pltpu.VMEM((3, STATE_ROWS, DH), F32),
            pltpu.VMEM((3, STATE_ROWS, DH), F32),
            pltpu.VMEM((3, 2, ROWS, DH), BF16),
            pltpu.VMEM((2, ROWS, DH), BF16),
            pltpu.VMEM((2, 2, ROWS, DH), BF16),
            pltpu.VMEM((2, ROWS, DH), F32),
            pltpu.VMEM((2, ROWS, DH), BF16),
            pltpu.VMEM((2, slot_rows, all_heads), BF16),
            pltpu.VMEM((X_RING, 8, DH), F32),
            pltpu.VMEM((max(n_ctx // X_RING, 1), 8, DH), F32),
            pltpu.VMEM((PER_GROUP * ROWS, DH), BF16),
            pltpu.VMEM((PER_GROUP * ROWS, DH), BF16),
            pltpu.VMEM((4, DH, ROWS), BF16),
            pltpu.VMEM((7 * TILE, TILE), F32),
            pltpu.VMEM((7 * TILE, TILE), F32),
            pltpu.VMEM((4, ROWS, PER_GROUP * ROWS), BF16),
            pltpu.VMEM((4, ROWS, PER_GROUP * ROWS), BF16),
            pltpu.VMEM((8, ROWS), F32),
            pltpu.VMEM((16, ROWS), F32),
            heads_wide,
            heads_wide,
            heads_wide,
            heads_wide,
            heads_wide,
            heads_wide,
            pltpu.VMEM((16, ROWS), F32),
            dma((8,)), dma((8,)), dma((4,)), dma((4,)), dma((6,)), dma((6,)), dma((4,)), dma((4,)),
            dma((8,)), dma((8,)), dma((4,)), dma((4,)), dma((8,)), dma((8,)),
        ],
        compiler_params=pltpu.CompilerParams(
            collective_id=0, has_side_effects=True, vmem_limit_bytes=56 * 1024 * 1024
        ),
    )(
        cross_query, cross_grad, cache_keys, cache_values, retention_query, retention_key,
        retention_value, retention_grad, log_decay, doc_offsets.reshape(1, -1),
    )


def solution(mesh):
    wide = P("ctx", "head")
    cache = P(("ctx", "head"), None)
    return jax.shard_map(
        on_device,
        mesh=mesh,
        in_specs=(wide, wide, cache, cache, wide, wide, wide, wide, P("head", "ctx"), P()),
        out_specs=(wide, cache, cache, wide, wide, wide, P("head", "ctx")),
        check_vma=False,
    )
```

```python
import jax
import jax.numpy as jnp
from jax import lax
from jax.experimental import pallas as pl
from jax.experimental.pallas import tpu as pltpu
from jax.sharding import PartitionSpec as P

ATTENDER_NUMBER = 24
KV_HEADS = 8
DH = 128
PER_GROUP = ATTENDER_NUMBER // KV_HEADS
ROWS = 512
TILE = 256
TILES = ROWS // TILE
X_RING = 4
SCALING = DH ** (-0.5)
EXPONENT_SCALE = SCALING * 1.4426950408889634
MESH = pl.DeviceIdType.MESH
BF16 = jnp.bfloat16
F32 = jnp.float32
STATE_ROWS = PER_GROUP * DH + 8


def matmul(a, b):
    return lax.dot_general(a, b, (((1,), (0,)), ((), ())), preferred_element_type=F32)


def matmul_nt(a, b):
    return lax.dot_general(a, b, (((1,), (1,)), ((), ())), preferred_element_type=F32)


def matmul_tn(a, b):
    return lax.dot_general(a, b, (((0,), (0,)), ((), ())), preferred_element_type=F32)


def exact_pieces(x):
    high = x.astype(BF16)
    rest = x - high.astype(F32)
    middle = rest.astype(BF16)
    low = (rest - middle.astype(F32)).astype(BF16)
    return jnp.concatenate([high, middle, low], axis=0)


def triangle_sum(x, triangle):
    parts = matmul(exact_pieces(x), triangle)
    return parts[0:16] + parts[16:32] + parts[32:48]


def body(
    n_ctx, n_head,
    cq, cg, ck, cv, rq, rk, rv, rg, ld, offs,
    gq, gk, gv, oq, ok, ov, dg,
    kvs, kvb, own_f, own_b, got_f, got_b, part, half, back, home, wait_sum, final, landed, tot_x, tot_z,
    qs, os, kt, score, dprob, prob_t, dscore_t,
    start_row, cum_row, cum_col, last_w, first_w, qf, kf, vf, pad16,
    head_s, head_r, kv_s, kv_r, st_s, st_r, gr_s, gr_r, fin_s, fin_r, tx_s, tx_r, tz_s, tz_r, ready,
):
    c = lax.axis_index("ctx")
    g = lax.axis_index("head")
    z_ring = n_ctx // X_RING
    slot_rows = ROWS // n_head

    def ctx_at(offset):
        return lax.rem(c + (offset + n_ctx), n_ctx)

    def head_at(offset):
        return lax.rem(g + offset, n_head)

    x = lax.rem(c, X_RING)
    z = c // X_RING

    def x_peer(offset):
        return z * X_RING + lax.rem(x + offset, X_RING)

    def z_peer(offset):
        return lax.rem(z + (offset + z_ring), z_ring) * X_RING + x

    def send(src, dst, send_sem, recv_sem, device):
        return pltpu.make_async_remote_copy(
            src_ref=src, dst_ref=dst, send_sem=send_sem, recv_sem=recv_sem,
            device_id=device, device_id_type=MESH,
        )

    def has(offset):
        if offset > 0:
            return c < n_ctx - offset
        return c >= -offset

    def z_has(offset):
        if offset > 0:
            return z < z_ring - offset
        return z >= -offset

    def start(transfer):
        pl.when(transfer[1])(lambda: transfer[0].start())

    def receive(transfer):
        pl.when(transfer[2])(lambda: transfer[0].wait_recv())

    def sent(transfer):
        pl.when(transfer[1])(lambda: transfer[0].wait_send())

    def clear(condition, ref):
        @pl.when(condition)
        def _():
            ref[...] = jnp.zeros(ref.shape, ref.dtype)

    barrier = pltpu.get_barrier_semaphore()
    greetings = n_head - 1 + X_RING - 1
    for k in range(1, n_head):
        pl.semaphore_signal(barrier, inc=1, device_id=(c, head_at(k)), device_id_type=MESH)
    for k in range(1, X_RING):
        pl.semaphore_signal(barrier, inc=1, device_id=(x_peer(k), g), device_id_type=MESH)
    for k in (1, -1, 3, -3):
        @pl.when(has(k))
        def _():
            pl.semaphore_signal(barrier, inc=1, device_id=(ctx_at(k), g), device_id_type=MESH)

        greetings = greetings + has(k).astype(jnp.int32)
    for k in (1, -1):
        if z_ring > 1:
            @pl.when(z_has(k))
            def _():
                pl.semaphore_signal(barrier, inc=1, device_id=(z_peer(k), g), device_id_type=MESH)

            greetings = greetings + z_has(k).astype(jnp.int32)

    def ready_round(r):
        if r < z_ring - 1:
            if r > 1:
                pl.when(z >= r)(lambda: pl.semaphore_wait(ready.at[r - 1], 1))

            @pl.when((z >= r) & (z < z_ring - 1))
            def _():
                pl.semaphore_signal(
                    ready.at[r], inc=1, device_id=(z_peer(1), g), device_id_type=MESH
                )

    for d in (1, 2, 3):
        clear(c < d, kvb.at[d])
        clear(c < d, got_f.at[d - 1])
        clear(c >= n_ctx - d, got_b.at[d - 1])
    clear((c == 0) | (c == n_ctx - 1), half.at[0])
    clear(c < 3, half.at[1])
    clear(c != n_ctx - 2, half.at[2])
    clear(c >= n_ctx - 1, back.at[0])
    clear(c >= n_ctx - 3, back.at[1])

    kvs[0] = ck[...]
    kvs[1] = cv[...]
    base = (c * ROWS).astype(F32)
    offsets = offs[...].astype(F32)
    pos_col = lax.broadcasted_iota(jnp.int32, (ROWS, 1), 0).astype(F32)
    begun = jnp.where(offsets <= pos_col + base, offsets, 0.0)
    start_col = jnp.max(begun, axis=1, keepdims=True) - base
    start_row[...] = jnp.broadcast_to(start_col, (ROWS, DH)).T[0:8]
    start_last = start_col[ROWS - 1 : ROWS, :]
    row_at = lax.broadcasted_iota(jnp.int32, (ROWS, ROWS), 0)
    col_at = lax.broadcasted_iota(jnp.int32, (ROWS, ROWS), 1)

    pad16[...] = jnp.zeros_like(pad16)
    pad16[0:PER_GROUP, :] = ld[...]
    cum = triangle_sum(pad16[...], (row_at <= col_at).astype(F32).astype(BF16))
    cum_row[...] = cum
    cum_t = jnp.concatenate([cum, jnp.zeros((DH - 16, ROWS), F32)], axis=0).T
    pl.semaphore_wait(barrier, greetings)

    head_copies = []
    for k in range(1, n_head):
        to = head_at(k)
        copy = send(
            kvs.at[:, :, pl.ds(pl.multiple_of(to * DH, DH), DH)],
            kvb.at[0, :, pl.ds(pl.multiple_of(g * slot_rows, slot_rows), slot_rows), :],
            head_s.at[k], head_r.at[k], (c, to),
        )
        copy.start()
        head_copies.append(copy)
    kvb[0, :, pl.ds(pl.multiple_of(g * slot_rows, slot_rows), slot_rows), :] = kvs[
        :, :, pl.ds(pl.multiple_of(g * DH, DH), DH)
    ]

    ready_round(1)

    carry_rows = []
    for h in range(PER_GROUP):
        lanes = slice(h * DH, (h + 1) * DH)
        col = cum_t[:, h : h + 1]
        final_cum = col[ROWS - 1 : ROWS, :]
        last = jnp.where(pos_col >= start_last, jnp.exp(final_cum - col), 0.0)
        first = jnp.where(start_col < 0.0, jnp.exp(col), 0.0) * SCALING
        cum_col[h] = jnp.broadcast_to(col, (ROWS, DH))
        last = jnp.broadcast_to(last, (ROWS, DH))
        first = jnp.broadcast_to(first, (ROWS, DH))
        last_w[h] = last
        first_w[h] = first
        keys_w = (last * rk[:, lanes].astype(F32)).astype(BF16)
        queries_w = (first * rq[:, lanes].astype(F32)).astype(BF16)
        own_f[h * DH : (h + 1) * DH, :] = matmul_tn(keys_w, rv[:, lanes])
        own_b[h * DH : (h + 1) * DH, :] = matmul_tn(queries_w, rg[:, lanes])
        carry = jnp.where(start_last < 0.0, jnp.exp(final_cum), 0.0)
        carry_rows.append(jnp.broadcast_to(carry, (8, DH)))
    which = lax.broadcasted_iota(jnp.int32, (8, DH), 0)
    carries = jnp.zeros((8, DH), F32)
    for h in range(PER_GROUP):
        carries = jnp.where(which == h, carry_rows[h], carries)
    own_f[PER_GROUP * DH :, :] = carries
    own_b[PER_GROUP * DH :, :] = carries

    for copy in head_copies:
        copy.wait_recv()
    up, down = (ctx_at(1), g), (ctx_at(-1), g)
    far_up, far_down = (ctx_at(3), g), (ctx_at(-3), g)

    def transfer(sems, n, src, dst, device, sends, receives):
        return send(src, dst, sems[0].at[n], sems[1].at[n], device), sends, receives

    kv_sems, st_sems, gr_sems = (kv_s, kv_r), (st_s, st_r), (gr_s, gr_r)
    kv_copies = [
        transfer(kv_sems, 0, kvb.at[0, 0], kvb.at[1, 0], up, has(1), has(-1)),
        transfer(kv_sems, 1, kvb.at[0, 1], kvb.at[3, 1], far_up, has(3), has(-3)),
        transfer(kv_sems, 2, kvb.at[0, 1], kvb.at[1, 1], up, has(1), has(-1)),
        transfer(kv_sems, 3, kvb.at[0, 0], kvb.at[3, 0], far_up, has(3), has(-3)),
        transfer(kv_sems, 4, kvb.at[1, 0], kvb.at[2, 0], up, has(1) & has(-1), has(-2)),
        transfer(
            kv_sems, 5, kvb.at[3, 1], kvb.at[2, 1], down, has(-3), (c >= 2) & (c < n_ctx - 1)
        ),
        transfer(kv_sems, 6, kvb.at[1, 1], kvb.at[2, 1], up, c == n_ctx - 2, c == n_ctx - 1),
    ]
    state_copies = [
        transfer(st_sems, 0, own_f, got_f.at[0], up, has(1), has(-1)),
        transfer(st_sems, 1, own_b, got_b.at[0], down, has(-1), has(1)),
        transfer(st_sems, 2, own_f, got_f.at[2], far_up, has(3), has(-3)),
        transfer(st_sems, 3, own_b, got_b.at[2], far_down, has(-3), has(3)),
        transfer(st_sems, 4, got_f.at[0], got_f.at[1], up, has(1) & has(-1), has(-2)),
        transfer(st_sems, 5, got_b.at[0], got_b.at[1], down, has(1) & has(-1), has(2)),
    ]
    for copy in kv_copies[:4]:
        start(copy)
    ready_round(2)

    for i in range(TILES):
        for h in range(PER_GROUP):
            at = (i * PER_GROUP + h) * TILE
            qs[at : at + TILE, :] = cq[i * TILE : (i + 1) * TILE, h * DH : (h + 1) * DH]
            os[at : at + TILE, :] = cg[i * TILE : (i + 1) * TILE, h * DH : (h + 1) * DH]

    tile_row = lax.broadcasted_iota(jnp.int32, (TILE, TILE), 0)
    tile_col = lax.broadcasted_iota(jnp.int32, (TILE, TILE), 1)
    tile_pos = tile_row.astype(F32)
    causal = tile_row <= tile_col

    def retention_head(h, nothing):
        lanes = pl.ds(pl.multiple_of(h * DH, DH), DH)
        for ti in range(TILES):
            t = slice(ti * TILE, (ti + 1) * TILE)
            rq_t = rq[t, lanes]
            rg_t = rg[t, lanes]
            cum_t_row = cum_row[pl.ds(h, 1), t]
            query_t = jnp.zeros((DH, TILE), F32)
            for si in range(ti + 1):
                s = slice(si * TILE, (si + 1) * TILE)
                rk_s = rk[s, lanes]
                allowed = tile_pos >= start_row[0:1, t] - float(si * TILE)
                if si == ti:
                    allowed = allowed & causal
                gap = jnp.minimum(cum_t_row - cum_col[h, s, 0:1], 0.0)
                within = jnp.where(allowed, jnp.exp(gap) * SCALING, 0.0)
                grad_w = (within * matmul_nt(rv[s, lanes], rg_t)).astype(BF16)
                score_w = (within * matmul_nt(rk_s, rq_t)).astype(BF16)
                query_t = query_t + matmul_tn(rk_s, grad_w)
                key_term = matmul(grad_w, rq_t)
                value_term = matmul(score_w, rg_t)
                if si == ti:
                    kf[h, s, :] = key_term
                    vf[h, s, :] = value_term
                else:
                    kf[h, s, :] = kf[h, s, :] + key_term
                    vf[h, s, :] = vf[h, s, :] + value_term
            qf[h, t, :] = query_t.T

        return nothing

    lax.fori_loop(0, PER_GROUP, retention_head, 0)

    for n in (0, 1):
        receive(kv_copies[n])
    start(kv_copies[4])
    start(kv_copies[5])
    receive(kv_copies[2])
    start(kv_copies[6])
    receive(kv_copies[3])
    ready_round(3)
    for d in (0, 1, 3):
        kt[d] = kvb[d, 0].astype(F32).T.astype(BF16)
    for n in (4, 5, 6):
        receive(kv_copies[n])
    kt[2] = kvb[2, 0].astype(F32).T.astype(BF16)
    start(state_copies[0])
    start(state_copies[1])

    def attention_head(h, nothing):
        for i in range(TILES):
            cols = pl.ds(pl.multiple_of(i * (PER_GROUP * TILE) + h * TILE, TILE), TILE)
            query = qs[cols, :]
            upstream = os[cols, :]
            start_t = start_row[0:1, i * TILE : (i + 1) * TILE]
            pieces = [(0, j) for j in range(i + 1)]
            pieces += [(d, j) for d in (1, 2) for j in range(TILES)]
            pieces += [(3, j) for j in range(i, TILES)]
            top = jnp.full((1, TILE), -1e30, F32)
            for n, (d, j) in enumerate(pieces):
                s = slice(j * TILE, (j + 1) * TILE)
                raw = matmul_nt(kvb[d, 0, s, :], query)
                allowed = tile_pos >= start_t + float(d * ROWS - j * TILE)
                if d == 0 and j == i:
                    allowed = allowed & causal
                raw = jnp.where(allowed, raw, -1e30)
                score[n * TILE : (n + 1) * TILE, :] = raw
                top = jnp.maximum(top, jnp.max(raw, axis=0, keepdims=True))
            total = jnp.zeros((1, TILE), F32)
            for n in range(len(pieces)):
                at = slice(n * TILE, (n + 1) * TILE)
                term = jnp.exp2((score[at, :] - top) * EXPONENT_SCALE)
                score[at, :] = term
                total = total + jnp.sum(term, axis=0, keepdims=True)
            inverse = 1.0 / total
            row_dot = jnp.zeros((1, TILE), F32)
            for n, (d, j) in enumerate(pieces):
                s = slice(j * TILE, (j + 1) * TILE)
                at = slice(n * TILE, (n + 1) * TILE)
                weights = score[at, :] * inverse
                weights_b = weights.astype(BF16)
                dweights = matmul_nt(kvb[d, 1, s, :], upstream)
                score[at, :] = weights
                dprob[at, :] = dweights
                prob_t[d, s, cols] = weights_b
                row_dot = row_dot + jnp.sum(weights_b.astype(F32) * dweights, axis=0, keepdims=True)
            query_t = jnp.zeros((DH, TILE), F32)
            for n, (d, j) in enumerate(pieces):
                s = slice(j * TILE, (j + 1) * TILE)
                at = slice(n * TILE, (n + 1) * TILE)
                dscores_b = (score[at, :] * (dprob[at, :] - row_dot)).astype(BF16)
                dscore_t[d, s, cols] = dscores_b
                query_t = query_t + matmul(kt[d, :, s], dscores_b)
            gq[i * TILE : (i + 1) * TILE, pl.ds(pl.multiple_of(h * DH, DH), DH)] = (
                query_t.T * SCALING
            ).astype(BF16)

        @pl.when(h == 0)
        def _():
            start(state_copies[2])
            start(state_copies[3])
            ready_round(4)

        @pl.when(h == 1)
        def _():
            receive(state_copies[0])
            start(state_copies[4])
            receive(state_copies[1])
            start(state_copies[5])
            ready_round(5)

        return nothing

    lax.fori_loop(0, PER_GROUP, attention_head, 0)

    width = PER_GROUP * TILE

    def partial_at(d, j):
        cols = slice(0, TILES * width)
        if d == 0:
            cols = slice(j * width, TILES * width)
        if d == 3:
            cols = slice(0, (j + 1) * width)
        return slice(j * TILE, (j + 1) * TILE), cols

    middle_device = has(1) & has(-1)
    grad_copies = [
        transfer(gr_sems, 0, part.at[1, 0], half.at[0], down, has(-2), middle_device),
        transfer(gr_sems, 1, part.at[1, 1], half.at[1], up, has(-2) & has(1), has(-3)),
        transfer(gr_sems, 2, part.at[1, 1], half.at[2], down, c == n_ctx - 1, c == n_ctx - 2),
        transfer(gr_sems, 3, part.at[2, 0], back.at[1, 0], far_down, has(-3), has(3)),
        transfer(gr_sems, 4, part.at[0, 1], back.at[0, 1], down, has(-1), has(1)),
        transfer(gr_sems, 5, part.at[2, 1], back.at[1, 1], far_down, has(-3), has(3)),
        transfer(gr_sems, 6, part.at[0, 0], back.at[0, 0], down, has(-1), has(1)),
    ]

    def key_grad(d, out, at):
        for j in range(TILES):
            s, cols = partial_at(d, j)
            value = matmul(dscore_t[d, s, cols], qs[cols, :]) * SCALING
            out[at + (s,)] = value.astype(out.dtype)

    def value_grad(d, out, at):
        for j in range(TILES):
            s, cols = partial_at(d, j)
            value = matmul(prob_t[d, s, cols], os[cols, :])
            out[at + (s,)] = value.astype(out.dtype)

    key_grad(2, part, (1, 0))
    start(grad_copies[0])
    value_grad(2, part, (1, 1))
    start(grad_copies[1])
    start(grad_copies[2])
    key_grad(3, part, (2, 0))
    start(grad_copies[3])
    value_grad(1, wait_sum, (0,))

    receive(grad_copies[2])

    part[0, 1] = (wait_sum[0] + half[2].astype(F32)).astype(BF16)
    start(grad_copies[4])
    value_grad(3, wait_sum, (1,))
    key_grad(1, wait_sum, (2,))
    key_grad(0, home, (0,))
    value_grad(0, home, (1,))
    ready_round(6)

    for copy in state_copies[2:]:
        receive(copy)
    sums = jnp.zeros((ROWS, DH), F32)
    lane_at = lax.broadcasted_iota(jnp.int32, (ROWS, DH), 1)
    for h in range(PER_GROUP):
        lanes = slice(h * DH, (h + 1) * DH)
        block = slice(h * DH, (h + 1) * DH)
        carry_at = slice(PER_GROUP * DH + h, PER_GROUP * DH + h + 1)

        def chained(got):
            inner = got[1, block, :] + got[1, carry_at, :] * got[2, block, :]
            return (got[0, block, :] + got[0, carry_at, :] * inner).astype(BF16)

        state_b = jnp.where(c > 0, chained(got_f), jnp.zeros((DH, DH), BF16))
        later_b = jnp.where(c < n_ctx - 1, chained(got_b), jnp.zeros((DH, DH), BF16))
        last = last_w[h]
        query_f = qf[h] + first_w[h] * matmul_nt(rg[:, lanes], state_b)
        key_f = kf[h] + last * matmul_nt(rv[:, lanes], later_b)
        value_f = vf[h] + last * matmul(rk[:, lanes], later_b)
        oq[:, lanes] = query_f.astype(BF16)
        ok[:, lanes] = key_f.astype(BF16)
        ov[:, lanes] = value_f.astype(BF16)
        residue = jnp.sum(rq[:, lanes].astype(F32) * query_f, axis=1, keepdims=True) - jnp.sum(
            rk[:, lanes].astype(F32) * key_f, axis=1, keepdims=True
        )
        sums = jnp.where(lane_at == h, residue, sums)
    suffix = triangle_sum(sums.T[0:16], (row_at >= col_at).astype(F32).astype(BF16))
    cum_row[...] = suffix
    tot_x[0] = jnp.broadcast_to(suffix[0:8, 0:1], (8, DH))
    x_copies = [
        send(tot_x.at[0], tot_x.at[k], tx_s.at[k], tx_r.at[k], (x_peer(k), g))
        for k in range(1, X_RING)
    ]
    for copy in x_copies:
        copy.start()

    receive(grad_copies[1])
    part[2, 1] = (wait_sum[1] + half[1].astype(F32)).astype(BF16)
    start(grad_copies[5])
    receive(grad_copies[0])
    part[0, 0] = (wait_sum[2] + half[0].astype(F32)).astype(BF16)
    start(grad_copies[6])

    for copy in x_copies:
        copy.wait_recv()
    row_total = tot_x[0]
    tail = jnp.zeros((8, DH), F32)
    for k in range(1, X_RING):
        row_total = row_total + tot_x[k]
        tail = tail + jnp.where(lax.rem(x - k + X_RING, X_RING) > x, tot_x[k], 0.0)
    tot_z[0] = row_total
    z_copies = [
        transfer((tz_s, tz_r), k, tot_z.at[0], tot_z.at[k], (z_peer(-k), g), z_has(-k), z_has(k))
        for k in range(1, z_ring)
    ]
    if z_ring > 2:
        pl.when(z >= z_ring - 1)(lambda: pl.semaphore_wait(ready.at[z_ring - 2], 1))
    for copy in z_copies:
        start(copy)

    for n in (3, 4, 5, 6):
        receive(grad_copies[n])
    for m in range(2):
        total = home[m] + back[0, m].astype(F32) + back[1, m].astype(F32)
        final[m] = total.astype(BF16)
    final_copies = []
    for k in range(1, n_head):
        to = head_at(k)
        copy = send(
            final.at[:, pl.ds(pl.multiple_of(to * slot_rows, slot_rows), slot_rows), :],
            landed.at[:, :, pl.ds(pl.multiple_of(g * DH, DH), DH)],
            fin_s.at[k], fin_r.at[k], (c, to),
        )
        copy.start()
        final_copies.append(copy)
    landed[:, :, pl.ds(pl.multiple_of(g * DH, DH), DH)] = final[
        :, pl.ds(pl.multiple_of(g * slot_rows, slot_rows), slot_rows), :
    ]

    for copy in z_copies:
        receive(copy)
    for k in range(1, z_ring):
        tail = tail + jnp.where(z_has(k), tot_z[k], 0.0)
    dg[...] = (cum_row[0:8, :] + tail[:, 0:1])[0:PER_GROUP]

    for copy in final_copies:
        copy.wait_recv()
    gk[...] = landed[0]
    gv[...] = landed[1]
    for copy in head_copies + x_copies + final_copies:
        copy.wait_send()
    for copy in kv_copies + state_copies + grad_copies + z_copies:
        sent(copy)


def write_out(*refs):
    count = 7
    sources, targets, held = refs[:count], refs[count : 2 * count], refs[2 * count : 3 * count]
    sem_in, sem_out = refs[3 * count :]
    loads = [pltpu.make_async_copy(sources[n], held[n], sem_in.at[n]) for n in range(count)]
    stores = [pltpu.make_async_copy(held[n], targets[n], sem_out.at[n]) for n in range(count)]
    for load in loads:
        load.start()
    for load, store in zip(loads, stores):
        load.wait()
        store.start()
    for store in stores:
        store.wait()


def on_device(
    cross_query, cross_grad, cache_keys, cache_values, retention_query, retention_key,
    retention_value, retention_grad, log_decay, doc_offsets,
):
    n_ctx = lax.axis_size("ctx")
    n_head = lax.axis_size("head")
    wide = jax.ShapeDtypeStruct(cross_query.shape, BF16)
    cache = jax.ShapeDtypeStruct(cache_keys.shape, BF16)
    vmem = pl.BlockSpec(memory_space=pltpu.VMEM)
    slot_rows, all_heads = cache_keys.shape
    dma = pltpu.SemaphoreType.DMA
    any_space = pl.BlockSpec(memory_space=pl.ANY)
    heads_wide = pltpu.VMEM((PER_GROUP, ROWS, DH), F32)
    results = pl.pallas_call(
        lambda *refs: body(n_ctx, n_head, *refs),
        out_shape=(
            wide, cache, cache, wide, wide, wide, jax.ShapeDtypeStruct(log_decay.shape, F32),
        ),
        in_specs=[vmem] * 10,
        out_specs=(vmem,) * 7,
        scratch_shapes=[
            pltpu.VMEM((2, slot_rows, all_heads), BF16),
            pltpu.VMEM((4, 2, ROWS, DH), BF16),
            pltpu.VMEM((STATE_ROWS, DH), F32),
            pltpu.VMEM((STATE_ROWS, DH), F32),
            pltpu.VMEM((3, STATE_ROWS, DH), F32),
            pltpu.VMEM((3, STATE_ROWS, DH), F32),
            pltpu.VMEM((3, 2, ROWS, DH), BF16),
            pltpu.VMEM((3, ROWS, DH), BF16),
            pltpu.VMEM((2, 2, ROWS, DH), BF16),
            pltpu.VMEM((2, ROWS, DH), F32),
            pltpu.VMEM((3, ROWS, DH), F32),
            pltpu.VMEM((2, ROWS, DH), BF16),
            pltpu.VMEM((2, slot_rows, all_heads), BF16),
            pltpu.VMEM((X_RING, 8, DH), F32),
            pltpu.VMEM((max(n_ctx // X_RING, 1), 8, DH), F32),
            pltpu.VMEM((PER_GROUP * ROWS, DH), BF16),
            pltpu.VMEM((PER_GROUP * ROWS, DH), BF16),
            pltpu.VMEM((4, DH, ROWS), BF16),
            pltpu.VMEM((7 * TILE, TILE), F32),
            pltpu.VMEM((7 * TILE, TILE), F32),
            pltpu.VMEM((4, ROWS, PER_GROUP * ROWS), BF16),
            pltpu.VMEM((4, ROWS, PER_GROUP * ROWS), BF16),
            pltpu.VMEM((8, ROWS), F32),
            pltpu.VMEM((16, ROWS), F32),
            heads_wide,
            heads_wide,
            heads_wide,
            heads_wide,
            heads_wide,
            heads_wide,
            pltpu.VMEM((16, ROWS), F32),
            dma((8,)), dma((8,)), dma((7,)), dma((7,)), dma((6,)), dma((6,)), dma((7,)), dma((7,)),
            dma((8,)), dma((8,)), dma((4,)), dma((4,)), dma((8,)), dma((8,)),
            pltpu.SemaphoreType.REGULAR((8,)),
        ],
        compiler_params=pltpu.CompilerParams(
            collective_id=0, has_side_effects=True, vmem_limit_bytes=56 * 1024 * 1024
        ),
    )(
        cross_query, cross_grad, cache_keys, cache_values, retention_query, retention_key,
        retention_value, retention_grad, log_decay, doc_offsets.reshape(1, -1),
    )
    return pl.pallas_call(
        write_out,
        out_shape=tuple(jax.ShapeDtypeStruct(r.shape, r.dtype) for r in results),
        in_specs=[any_space] * 7,
        out_specs=(any_space,) * 7,
        scratch_shapes=[pltpu.VMEM(r.shape, r.dtype) for r in results] + [dma((7,)), dma((7,))],
    )(*results)


def solution(mesh):
    wide = P("ctx", "head")
    cache = P(("ctx", "head"), None)
    return jax.shard_map(
        on_device,
        mesh=mesh,
        in_specs=(wide, wide, cache, cache, wide, wide, wide, wide, P("head", "ctx"), P()),
        out_specs=(wide, cache, cache, wide, wide, wide, P("head", "ctx")),
        check_vma=False,
    )
```

```python
import jax
import jax.numpy as jnp
from jax import lax
from jax.experimental import pallas as pl
from jax.experimental.pallas import tpu as pltpu
from jax.sharding import PartitionSpec as P

ATTENDER_NUMBER = 24
KV_HEADS = 8
DH = 128
PER_GROUP = ATTENDER_NUMBER // KV_HEADS
ROWS = 512
TILE = 256
TILES = ROWS // TILE
DOC_BLOCKS = 4
STRIP = 128
X_RING = 4
SCALING = DH ** (-0.5)
EXPONENT_SCALE = SCALING * 1.4426950408889634
MESH = pl.DeviceIdType.MESH
BF16 = jnp.bfloat16
F32 = jnp.float32
STATE_ROWS = PER_GROUP * DH + 8


def matmul(a, b):
    return lax.dot_general(a, b, (((1,), (0,)), ((), ())), preferred_element_type=F32)


def matmul_nt(a, b):
    return lax.dot_general(a, b, (((1,), (1,)), ((), ())), preferred_element_type=F32)


def matmul_tn(a, b):
    return lax.dot_general(a, b, (((0,), (0,)), ((), ())), preferred_element_type=F32)


def exact_pieces(x):
    high = x.astype(BF16)
    rest = x - high.astype(F32)
    middle = rest.astype(BF16)
    low = (rest - middle.astype(F32)).astype(BF16)
    return jnp.concatenate([high, middle, low], axis=0)


def triangle_sum(x, triangle):
    parts = matmul(exact_pieces(x), triangle)
    return parts[0:16] + parts[16:32] + parts[32:48]


def body(
    n_ctx, n_head,
    cq, cg, ck, cv, rq, rk, rv, rg, ld, offs,
    gq, gk, gv, oq, ok, ov, dg,
    kvs, kvb, kv_thru, own_f, own_b, got_f, got_b, thru, part, half, back, grad_thru, home, wait_sum, final, landed, tot_x, tot_z,
    qs, os, kt, score, dprob, tops, prob_t, dscore_t,
    start_row, cum_row, cum_col, last_w, first_w, qf, kf, vf, pad16,
    head_s, head_r, kv_s, kv_r, st_s, st_r, gr_s, gr_r, fin_s, fin_r, tx_s, tx_r, tz_s, tz_r, ready,
):
    c = lax.axis_index("ctx")
    g = lax.axis_index("head")
    z_ring = n_ctx // X_RING
    slot_rows = ROWS // n_head

    def ctx_at(offset):
        return lax.rem(c + (offset + n_ctx), n_ctx)

    def head_at(offset):
        return lax.rem(g + offset, n_head)

    x = lax.rem(c, X_RING)
    z = c // X_RING

    def x_peer(offset):
        return z * X_RING + lax.rem(x + offset, X_RING)

    def z_peer(offset):
        return lax.rem(z + (offset + z_ring), z_ring) * X_RING + x

    def send(src, dst, send_sem, recv_sem, device):
        return pltpu.make_async_remote_copy(
            src_ref=src, dst_ref=dst, send_sem=send_sem, recv_sem=recv_sem,
            device_id=device, device_id_type=MESH,
        )

    def has(offset):
        if offset > 0:
            return c < n_ctx - offset
        return c >= -offset

    def z_has(offset):
        if offset > 0:
            return z < z_ring - offset
        return z >= -offset

    def start(transfer):
        pl.when(transfer[1])(lambda: transfer[0].start())

    def receive(transfer):
        pl.when(transfer[2])(lambda: transfer[0].wait_recv())

    def sent(transfer):
        pl.when(transfer[1])(lambda: transfer[0].wait_send())

    def clear(condition, ref):
        @pl.when(condition)
        def _():
            ref[...] = jnp.zeros(ref.shape, ref.dtype)

    barrier = pltpu.get_barrier_semaphore()
    greetings = n_head - 1 + X_RING - 1
    for k in range(1, n_head):
        pl.semaphore_signal(barrier, inc=1, device_id=(c, head_at(k)), device_id_type=MESH)
    for k in range(1, X_RING):
        pl.semaphore_signal(barrier, inc=1, device_id=(x_peer(k), g), device_id_type=MESH)
    for k in (1, -1, 3, -3):
        @pl.when(has(k))
        def _():
            pl.semaphore_signal(barrier, inc=1, device_id=(ctx_at(k), g), device_id_type=MESH)

        greetings = greetings + has(k).astype(jnp.int32)
    for k in (1, -1):
        if z_ring > 1:
            @pl.when(z_has(k))
            def _():
                pl.semaphore_signal(barrier, inc=1, device_id=(z_peer(k), g), device_id_type=MESH)

            greetings = greetings + z_has(k).astype(jnp.int32)

    def ready_round(r):
        if r < z_ring - 1:
            if r > 1:
                pl.when(z >= r)(lambda: pl.semaphore_wait(ready.at[r - 1], 1))

            @pl.when((z >= r) & (z < z_ring - 1))
            def _():
                pl.semaphore_signal(
                    ready.at[r], inc=1, device_id=(z_peer(1), g), device_id_type=MESH
                )

    for d in (1, 2, 3):
        clear(c < d, kvb.at[d])
        clear(c < d, got_f.at[d - 1])
        clear(c >= n_ctx - d, got_b.at[d - 1])
    clear((c == 0) | (c == n_ctx - 1), half.at[0])
    clear(c < 3, half.at[1])
    clear(c != n_ctx - 2, half.at[2])
    clear(c >= n_ctx - 1, back.at[0])
    clear(c >= n_ctx - 3, back.at[1])

    kvs[0] = ck[...]
    kvs[1] = cv[...]
    base = (c * ROWS).astype(F32)
    offsets = offs[...].astype(F32)
    pos_col = lax.broadcasted_iota(jnp.int32, (ROWS, 1), 0).astype(F32)
    begun = jnp.where(offsets <= pos_col + base, offsets, 0.0)
    start_col = jnp.max(begun, axis=1, keepdims=True) - base
    start_row[...] = jnp.broadcast_to(start_col, (ROWS, DH)).T[0:8]
    start_last = start_col[ROWS - 1 : ROWS, :]
    row_at = lax.broadcasted_iota(jnp.int32, (ROWS, ROWS), 0)
    col_at = lax.broadcasted_iota(jnp.int32, (ROWS, ROWS), 1)

    pad16[...] = jnp.zeros_like(pad16)
    pad16[0:PER_GROUP, :] = ld[...]
    cum = triangle_sum(pad16[...], (row_at <= col_at).astype(F32).astype(BF16))
    cum_row[...] = cum
    cum_t = jnp.concatenate([cum, jnp.zeros((DH - 16, ROWS), F32)], axis=0).T
    pl.semaphore_wait(barrier, greetings)

    head_copies = []
    for k in range(1, n_head):
        to = head_at(k)
        copy = send(
            kvs.at[:, :, pl.ds(pl.multiple_of(to * DH, DH), DH)],
            kvb.at[0, :, pl.ds(pl.multiple_of(g * slot_rows, slot_rows), slot_rows), :],
            head_s.at[k], head_r.at[k], (c, to),
        )
        copy.start()
        head_copies.append(copy)
    kvb[0, :, pl.ds(pl.multiple_of(g * slot_rows, slot_rows), slot_rows), :] = kvs[
        :, :, pl.ds(pl.multiple_of(g * DH, DH), DH)
    ]

    ready_round(1)

    carry_rows = []
    for h in range(PER_GROUP):
        lanes = slice(h * DH, (h + 1) * DH)
        col = cum_t[:, h : h + 1]
        final_cum = col[ROWS - 1 : ROWS, :]
        last = jnp.where(pos_col >= start_last, jnp.exp(final_cum - col), 0.0)
        first = jnp.where(start_col < 0.0, jnp.exp(col), 0.0) * SCALING
        cum_col[h] = jnp.broadcast_to(col, (ROWS, DH))
        last = jnp.broadcast_to(last, (ROWS, DH))
        first = jnp.broadcast_to(first, (ROWS, DH))
        last_w[h] = last
        first_w[h] = first
        keys_w = (last * rk[:, lanes].astype(F32)).astype(BF16)
        queries_w = (first * rq[:, lanes].astype(F32)).astype(BF16)
        own_f[h * DH : (h + 1) * DH, :] = matmul_tn(keys_w, rv[:, lanes])
        own_b[h * DH : (h + 1) * DH, :] = matmul_tn(queries_w, rg[:, lanes])
        carry = jnp.where(start_last < 0.0, jnp.exp(final_cum), 0.0)
        carry_rows.append(jnp.broadcast_to(carry, (8, DH)))
    which = lax.broadcasted_iota(jnp.int32, (8, DH), 0)
    carries = jnp.zeros((8, DH), F32)
    for h in range(PER_GROUP):
        carries = jnp.where(which == h, carry_rows[h], carries)
    own_f[PER_GROUP * DH :, :] = carries
    own_b[PER_GROUP * DH :, :] = carries

    for copy in head_copies:
        copy.wait_recv()
    up, down = (ctx_at(1), g), (ctx_at(-1), g)
    far_up, far_down = (ctx_at(3), g), (ctx_at(-3), g)

    def transfer(sems, n, src, dst, device, sends, receives):
        return send(src, dst, sems[0].at[n], sems[1].at[n], device), sends, receives

    kv_sems, st_sems, gr_sems = (kv_s, kv_r), (st_s, st_r), (gr_s, gr_r)
    over = (ctx_at(4), g)
    inner, outer = (c >= 1) & (x > 0), x == 0
    kv_copies = [
        transfer(kv_sems, 0, kvb.at[0, 0], kvb.at[1, 0], up, has(1) & (x < 3), inner),
        transfer(kv_sems, 1, kvb.at[0, 1], kvb.at[3, 1], far_up, has(3), has(-3)),
        transfer(kv_sems, 2, kvb.at[0, 1], kvb.at[1, 1], up, has(1) & (x < 3), inner),
        transfer(kv_sems, 3, kvb.at[0, 0], kvb.at[3, 0], far_up, has(3), has(-3)),
        transfer(kv_sems, 4, kvb.at[1, 0], kvb.at[2, 0], up, has(1) & inner, has(-2)),
        transfer(
            kv_sems, 5, kvb.at[3, 1], kvb.at[2, 1], down, has(-3), (c >= 2) & (c < n_ctx - 1)
        ),
        transfer(kv_sems, 6, kvb.at[1, 1], kvb.at[2, 1], up, c == n_ctx - 2, c == n_ctx - 1),
        transfer(kv_sems, 7, kvb.at[0, 0], kv_thru.at[0], far_down, (x == 3) & has(1), outer & has(4)),
        transfer(kv_sems, 8, kvb.at[0, 1], kv_thru.at[1], far_down, (x == 3) & has(1), outer & has(4)),
        transfer(kv_sems, 9, kv_thru.at[0], kvb.at[1, 0], over, outer & has(4), outer & has(-4)),
        transfer(kv_sems, 10, kv_thru.at[1], kvb.at[1, 1], over, outer & has(4), outer & has(-4)),
        transfer(kv_sems, 4, kvb.at[1, 0], kvb.at[2, 0], up, outer & has(1) & has(-4), has(-2)),
    ]
    state_copies = [
        transfer(st_sems, 0, own_f, got_f.at[0], up, has(1) & (x < 3), has(-1) & (x > 0)),
        transfer(st_sems, 1, own_b, got_b.at[0], down, has(-1), has(1)),
        transfer(st_sems, 2, own_f, got_f.at[2], far_up, has(3) & (x < 3), has(-3) & (x != 2)),
        transfer(st_sems, 3, own_b, got_b.at[2], far_down, has(-3), has(3)),
        transfer(st_sems, 4, got_f.at[0], got_f.at[1], up, has(1) & has(-1), has(-2)),
        transfer(st_sems, 5, got_b.at[0], got_b.at[1], down, has(1) & has(-1), has(2)),
        transfer(st_sems, 6, own_f, thru, far_down, (x == 3) & has(1), (x == 0) & has(4)),
        transfer(st_sems, 7, own_f, thru, down, (x == 3) & has(3), (x == 2) & has(4)),
        transfer(st_sems, 8, thru, got_f.at[0], over, (x == 0) & has(4), (x == 0) & has(-4)),
        transfer(st_sems, 9, thru, got_f.at[2], over, (x == 2) & has(4), (x == 2) & has(-4)),
    ]
    for n in (7, 0, 1, 8, 2, 3):
        start(kv_copies[n])
    ready_round(2)

    for i in range(TILES):
        for h in range(PER_GROUP):
            at = (i * PER_GROUP + h) * TILE
            qs[at : at + TILE, :] = cq[i * TILE : (i + 1) * TILE, h * DH : (h + 1) * DH]
            os[at : at + TILE, :] = cg[i * TILE : (i + 1) * TILE, h * DH : (h + 1) * DH]

    tile_row = lax.broadcasted_iota(jnp.int32, (TILE, TILE), 0)
    tile_col = lax.broadcasted_iota(jnp.int32, (TILE, TILE), 1)
    tile_pos = tile_row.astype(F32)
    causal = tile_row <= tile_col

    def retention_head(h, nothing):
        lanes = pl.ds(pl.multiple_of(h * DH, DH), DH)
        for ti in range(TILES):
            t = slice(ti * TILE, (ti + 1) * TILE)
            rq_t = rq[t, lanes]
            rg_t = rg[t, lanes]
            cum_t_row = cum_row[pl.ds(h, 1), t]
            query_t = jnp.zeros((DH, TILE), F32)
            for si in range(ti + 1):
                s = slice(si * TILE, (si + 1) * TILE)
                rk_s = rk[s, lanes]
                allowed = tile_pos >= start_row[0:1, t] - float(si * TILE)
                if si == ti:
                    allowed = allowed & causal
                gap = jnp.minimum(cum_t_row - cum_col[h, s, 0:1], 0.0)
                within = jnp.where(allowed, jnp.exp(gap) * SCALING, 0.0)
                grad_w = (within * matmul_nt(rv[s, lanes], rg_t)).astype(BF16)
                score_w = (within * matmul_nt(rk_s, rq_t)).astype(BF16)
                query_t = query_t + matmul_tn(rk_s, grad_w)
                key_term = matmul(grad_w, rq_t)
                value_term = matmul(score_w, rg_t)
                if si == ti:
                    kf[h, s, :] = key_term
                    vf[h, s, :] = value_term
                else:
                    kf[h, s, :] = kf[h, s, :] + key_term
                    vf[h, s, :] = vf[h, s, :] + value_term
            qf[h, t, :] = query_t.T

        return nothing

    lax.fori_loop(0, PER_GROUP, retention_head, 0)

    def tile_strips(i):
        strips = []
        for d in range(DOC_BLOCKS):
            first, stop = (0, (i + 1) * TILE) if d == 0 else (0, ROWS)
            if d == DOC_BLOCKS - 1:
                first = i * TILE
            strips += [(d, at) for at in range(first, stop, STRIP)]
        return strips

    def tile_columns(h, i):
        return pl.ds(pl.multiple_of(i * (PER_GROUP * TILE) + h * TILE, TILE), TILE)

    def scores_of_block(block):
        def one_head(h, nothing):
            for i in range(TILES):
                at_tile = h * TILES + i
                cols = tile_columns(h, i)
                query = qs[cols, :]
                upstream = os[cols, :]
                start_t = start_row[0:1, i * TILE : (i + 1) * TILE]
                top = jnp.full((8, TILE), -1e30, F32) if block == 0 else tops[at_tile]
                for n, (d, at_s) in enumerate(tile_strips(i)):
                    if d != block:
                        continue
                    s = slice(at_s, at_s + STRIP)
                    at = slice(n * STRIP, (n + 1) * STRIP)
                    raw = matmul_nt(kvb[d, 0, s, :], query)
                    allowed = strip_pos >= start_t + float(d * ROWS - at_s)
                    if d == 0 and at_s >= i * TILE:
                        allowed = allowed & (strip_row + (at_s - i * TILE) <= strip_col)
                    raw = jnp.where(allowed, raw, -1e30)
                    score[at_tile, at, :] = raw
                    top = jnp.maximum(top, jnp.max(raw.reshape(STRIP // 8, 8, TILE), axis=0))
                    dprob[at_tile, at, :] = matmul_nt(kvb[d, 1, s, :], upstream)
                tops[at_tile] = top
            return nothing

        lax.fori_loop(0, PER_GROUP, one_head, 0)

    strip_row = lax.broadcasted_iota(jnp.int32, (STRIP, TILE), 0)
    strip_col = lax.broadcasted_iota(jnp.int32, (STRIP, TILE), 1)
    strip_pos = strip_row.astype(F32)

    receive(kv_copies[7])
    start(kv_copies[9])
    for n in (0, 1):
        receive(kv_copies[n])
        start(kv_copies[n + 4])
    for n in (6, 7, 1, 0, 3, 2):
        start(state_copies[n])
    scores_of_block(0)
    receive(kv_copies[8])
    start(kv_copies[10])
    receive(kv_copies[2])
    start(kv_copies[6])
    receive(kv_copies[3])
    ready_round(3)
    scores_of_block(3)
    receive(kv_copies[9])
    start(kv_copies[11])
    receive(kv_copies[10])
    scores_of_block(1)
    for n in (6, 7):
        receive(state_copies[n])
        start(state_copies[n + 2])
    for d in (0, 1, 3):
        kt[d] = kvb[d, 0].astype(F32).T.astype(BF16)
    for n in (4, 5, 6):
        receive(kv_copies[n])
    kt[2] = kvb[2, 0].astype(F32).T.astype(BF16)
    receive(state_copies[1])
    start(state_copies[5])
    scores_of_block(2)
    receive(state_copies[0])
    receive(state_copies[8])
    start(state_copies[4])

    def attention_head(h, nothing):
        for i in range(TILES):
            at_tile = h * TILES + i
            cols = tile_columns(h, i)
            strips = tile_strips(i)
            top = jnp.max(tops[at_tile], axis=0, keepdims=True)
            total = jnp.zeros((8, TILE), F32)
            for n in range(len(strips)):
                at = slice(n * STRIP, (n + 1) * STRIP)
                term = jnp.exp2((score[at_tile, at, :] - top) * EXPONENT_SCALE)
                score[at_tile, at, :] = term
                total = total + jnp.sum(term.reshape(STRIP // 8, 8, TILE), axis=0)
            inverse = 1.0 / jnp.sum(total, axis=0, keepdims=True)
            row_dot = jnp.zeros((8, TILE), F32)
            for n, (d, at_s) in enumerate(strips):
                s = slice(at_s, at_s + STRIP)
                at = slice(n * STRIP, (n + 1) * STRIP)
                weights = score[at_tile, at, :] * inverse
                weights_b = weights.astype(BF16)
                prob_t[d, s, cols] = weights_b
                products = weights_b.astype(F32) * dprob[at_tile, at, :]
                row_dot = row_dot + jnp.sum(products.reshape(STRIP // 8, 8, TILE), axis=0)
            row_dot = jnp.sum(row_dot, axis=0, keepdims=True)
            query_t = jnp.zeros((DH, TILE), F32)
            for n, (d, at_s) in enumerate(strips):
                s = slice(at_s, at_s + STRIP)
                at = slice(n * STRIP, (n + 1) * STRIP)
                gaps = dprob[at_tile, at, :] - row_dot
                dscores_b = ((score[at_tile, at, :] * inverse) * gaps).astype(BF16)
                dscore_t[d, s, cols] = dscores_b
            for d in range(DOC_BLOCKS):
                first, stop = (0, (i + 1) * TILE) if d == 0 else (0, ROWS)
                if d == DOC_BLOCKS - 1:
                    first = i * TILE
                query_t = query_t + matmul(kt[d, :, first:stop], dscore_t[d, first:stop, cols])
            gq[i * TILE : (i + 1) * TILE, pl.ds(pl.multiple_of(h * DH, DH), DH)] = (
                query_t.T * SCALING
            ).astype(BF16)

        @pl.when(h == 0)
        def _():
            ready_round(4)

        @pl.when(h == 1)
        def _():
            ready_round(5)

        return nothing

    lax.fori_loop(0, PER_GROUP, attention_head, 0)

    width = PER_GROUP * TILE

    def partial_at(d, j):
        cols = slice(0, TILES * width)
        if d == 0:
            cols = slice(j * width, TILES * width)
        if d == 3:
            cols = slice(0, (j + 1) * width)
        return slice(j * TILE, (j + 1) * TILE), cols

    middle_device = has(1) & has(-1)
    grad_copies = [
        transfer(gr_sems, 0, part.at[1, 0], half.at[0], down, has(-2), middle_device),
        transfer(gr_sems, 1, part.at[1, 1], half.at[1], up, has(-2) & has(1), has(-3)),
        transfer(gr_sems, 2, part.at[1, 1], half.at[2], down, c == n_ctx - 1, c == n_ctx - 2),
        transfer(gr_sems, 3, part.at[2, 0], back.at[1, 0], far_down, has(-3), has(3)),
        transfer(
            gr_sems, 4, part.at[0, 1], back.at[0, 1], down, has(-1) & (x > 0), has(1) & (x < 3)
        ),
        transfer(gr_sems, 5, part.at[2, 1], back.at[1, 1], far_down, has(-3), has(3)),
        transfer(gr_sems, 6, part.at[0, 0], back.at[0, 0], down, has(-1), has(1)),
        transfer(gr_sems, 7, part.at[0, 1], grad_thru, far_up, (x == 0) & has(-4), (x == 3) & has(-4)),
        transfer(
            gr_sems, 8, grad_thru, back.at[0, 1], (ctx_at(-4), g), (x == 3) & has(-4), (x == 3) & has(4)
        ),
    ]

    def key_grad(d, out, at):
        for j in range(TILES):
            s, cols = partial_at(d, j)
            value = matmul(dscore_t[d, s, cols], qs[cols, :]) * SCALING
            out[at + (s,)] = value.astype(out.dtype)

    def value_grad(d, out, at):
        for j in range(TILES):
            s, cols = partial_at(d, j)
            value = matmul(prob_t[d, s, cols], os[cols, :])
            out[at + (s,)] = value.astype(out.dtype)

    key_grad(2, part, (1, 0))
    start(grad_copies[0])
    value_grad(2, part, (1, 1))
    start(grad_copies[1])
    start(grad_copies[2])
    key_grad(3, part, (2, 0))
    start(grad_copies[3])
    value_grad(1, wait_sum, (0,))

    receive(grad_copies[2])

    part[0, 1] = (wait_sum[0] + half[2].astype(F32)).astype(BF16)
    start(grad_copies[4])
    start(grad_copies[7])
    value_grad(3, wait_sum, (1,))
    key_grad(1, wait_sum, (2,))
    key_grad(0, home, (0,))
    value_grad(0, home, (1,))
    ready_round(6)

    for n in (2, 3, 4, 5, 9):
        receive(state_copies[n])
    sums = jnp.zeros((ROWS, DH), F32)
    lane_at = lax.broadcasted_iota(jnp.int32, (ROWS, DH), 1)
    for h in range(PER_GROUP):
        lanes = slice(h * DH, (h + 1) * DH)
        block = slice(h * DH, (h + 1) * DH)
        carry_at = slice(PER_GROUP * DH + h, PER_GROUP * DH + h + 1)

        def chained(got):
            inner = got[1, block, :] + got[1, carry_at, :] * got[2, block, :]
            return (got[0, block, :] + got[0, carry_at, :] * inner).astype(BF16)

        state_b = jnp.where(c > 0, chained(got_f), jnp.zeros((DH, DH), BF16))
        later_b = jnp.where(c < n_ctx - 1, chained(got_b), jnp.zeros((DH, DH), BF16))
        last = last_w[h]
        query_f = qf[h] + first_w[h] * matmul_nt(rg[:, lanes], state_b)
        key_f = kf[h] + last * matmul_nt(rv[:, lanes], later_b)
        value_f = vf[h] + last * matmul(rk[:, lanes], later_b)
        oq[:, lanes] = query_f.astype(BF16)
        ok[:, lanes] = key_f.astype(BF16)
        ov[:, lanes] = value_f.astype(BF16)
        residue = jnp.sum(rq[:, lanes].astype(F32) * query_f, axis=1, keepdims=True) - jnp.sum(
            rk[:, lanes].astype(F32) * key_f, axis=1, keepdims=True
        )
        sums = jnp.where(lane_at == h, residue, sums)
    suffix = triangle_sum(sums.T[0:16], (row_at >= col_at).astype(F32).astype(BF16))
    cum_row[...] = suffix
    tot_x[0] = jnp.broadcast_to(suffix[0:8, 0:1], (8, DH))
    x_copies = [
        send(tot_x.at[0], tot_x.at[k], tx_s.at[k], tx_r.at[k], (x_peer(k), g))
        for k in range(1, X_RING)
    ]
    for copy in x_copies:
        copy.start()

    receive(grad_copies[7])
    start(grad_copies[8])
    receive(grad_copies[1])
    part[2, 1] = (wait_sum[1] + half[1].astype(F32)).astype(BF16)
    start(grad_copies[5])
    receive(grad_copies[0])
    part[0, 0] = (wait_sum[2] + half[0].astype(F32)).astype(BF16)
    start(grad_copies[6])

    for copy in x_copies:
        copy.wait_recv()
    row_total = tot_x[0]
    tail = jnp.zeros((8, DH), F32)
    for k in range(1, X_RING):
        row_total = row_total + tot_x[k]
        tail = tail + jnp.where(lax.rem(x - k + X_RING, X_RING) > x, tot_x[k], 0.0)
    tot_z[0] = row_total
    z_copies = [
        transfer((tz_s, tz_r), k, tot_z.at[0], tot_z.at[k], (z_peer(-k), g), z_has(-k), z_has(k))
        for k in range(1, z_ring)
    ]
    if z_ring > 2:
        pl.when(z >= z_ring - 1)(lambda: pl.semaphore_wait(ready.at[z_ring - 2], 1))
    for copy in z_copies:
        start(copy)

    for n in (3, 4, 5, 6, 8):
        receive(grad_copies[n])
    for m in range(2):
        total = home[m] + back[0, m].astype(F32) + back[1, m].astype(F32)
        final[m] = total.astype(BF16)
    final_copies = []
    for k in range(1, n_head):
        to = head_at(k)
        copy = send(
            final.at[:, pl.ds(pl.multiple_of(to * slot_rows, slot_rows), slot_rows), :],
            landed.at[:, :, pl.ds(pl.multiple_of(g * DH, DH), DH)],
            fin_s.at[k], fin_r.at[k], (c, to),
        )
        copy.start()
        final_copies.append(copy)
    landed[:, :, pl.ds(pl.multiple_of(g * DH, DH), DH)] = final[
        :, pl.ds(pl.multiple_of(g * slot_rows, slot_rows), slot_rows), :
    ]

    for copy in z_copies:
        receive(copy)
    for k in range(1, z_ring):
        tail = tail + jnp.where(z_has(k), tot_z[k], 0.0)
    dg[...] = (cum_row[0:8, :] + tail[:, 0:1])[0:PER_GROUP]

    for copy in final_copies:
        copy.wait_recv()
    gk[...] = landed[0]
    gv[...] = landed[1]
    for copy in head_copies + x_copies + final_copies:
        copy.wait_send()
    for copy in kv_copies + state_copies + grad_copies + z_copies:
        sent(copy)


def write_out(*refs):
    count = 7
    sources, targets, held = refs[:count], refs[count : 2 * count], refs[2 * count : 3 * count]
    sem_in, sem_out = refs[3 * count :]
    loads = [pltpu.make_async_copy(sources[n], held[n], sem_in.at[n]) for n in range(count)]
    stores = [pltpu.make_async_copy(held[n], targets[n], sem_out.at[n]) for n in range(count)]
    for load in loads:
        load.start()
    for load, store in zip(loads, stores):
        load.wait()
        store.start()
    for store in stores:
        store.wait()


def on_device(
    cross_query, cross_grad, cache_keys, cache_values, retention_query, retention_key,
    retention_value, retention_grad, log_decay, doc_offsets,
):
    n_ctx = lax.axis_size("ctx")
    n_head = lax.axis_size("head")
    wide = jax.ShapeDtypeStruct(cross_query.shape, BF16)
    cache = jax.ShapeDtypeStruct(cache_keys.shape, BF16)
    vmem = pl.BlockSpec(memory_space=pltpu.VMEM)
    slot_rows, all_heads = cache_keys.shape
    dma = pltpu.SemaphoreType.DMA
    any_space = pl.BlockSpec(memory_space=pl.ANY)
    heads_wide = pltpu.VMEM((PER_GROUP, ROWS, DH), F32)
    results = pl.pallas_call(
        lambda *refs: body(n_ctx, n_head, *refs),
        out_shape=(
            wide, cache, cache, wide, wide, wide, jax.ShapeDtypeStruct(log_decay.shape, F32),
        ),
        in_specs=[vmem] * 10,
        out_specs=(vmem,) * 7,
        scratch_shapes=[
            pltpu.VMEM((2, slot_rows, all_heads), BF16),
            pltpu.VMEM((4, 2, ROWS, DH), BF16),
            pltpu.VMEM((2, ROWS, DH), BF16),
            pltpu.VMEM((STATE_ROWS, DH), F32),
            pltpu.VMEM((STATE_ROWS, DH), F32),
            pltpu.VMEM((3, STATE_ROWS, DH), F32),
            pltpu.VMEM((3, STATE_ROWS, DH), F32),
            pltpu.VMEM((STATE_ROWS, DH), F32),
            pltpu.VMEM((3, 2, ROWS, DH), BF16),
            pltpu.VMEM((3, ROWS, DH), BF16),
            pltpu.VMEM((2, 2, ROWS, DH), BF16),
            pltpu.VMEM((ROWS, DH), BF16),
            pltpu.VMEM((2, ROWS, DH), F32),
            pltpu.VMEM((3, ROWS, DH), F32),
            pltpu.VMEM((2, ROWS, DH), BF16),
            pltpu.VMEM((2, slot_rows, all_heads), BF16),
            pltpu.VMEM((X_RING, 8, DH), F32),
            pltpu.VMEM((max(n_ctx // X_RING, 1), 8, DH), F32),
            pltpu.VMEM((PER_GROUP * ROWS, DH), BF16),
            pltpu.VMEM((PER_GROUP * ROWS, DH), BF16),
            pltpu.VMEM((4, DH, ROWS), BF16),
            pltpu.VMEM((PER_GROUP * TILES, 7 * TILE, TILE), F32),
            pltpu.VMEM((PER_GROUP * TILES, 7 * TILE, TILE), F32),
            pltpu.VMEM((PER_GROUP * TILES, 8, TILE), F32),
            pltpu.VMEM((4, ROWS, PER_GROUP * ROWS), BF16),
            pltpu.VMEM((4, ROWS, PER_GROUP * ROWS), BF16),
            pltpu.VMEM((8, ROWS), F32),
            pltpu.VMEM((16, ROWS), F32),
            heads_wide,
            heads_wide,
            heads_wide,
            heads_wide,
            heads_wide,
            heads_wide,
            pltpu.VMEM((16, ROWS), F32),
            dma((8,)), dma((8,)), dma((11,)), dma((11,)), dma((10,)), dma((10,)), dma((9,)), dma((9,)),
            dma((8,)), dma((8,)), dma((4,)), dma((4,)), dma((8,)), dma((8,)),
            pltpu.SemaphoreType.REGULAR((8,)),
        ],
        compiler_params=pltpu.CompilerParams(
            collective_id=0, has_side_effects=True, vmem_limit_bytes=56 * 1024 * 1024
        ),
    )(
        cross_query, cross_grad, cache_keys, cache_values, retention_query, retention_key,
        retention_value, retention_grad, log_decay, doc_offsets.reshape(1, -1),
    )
    return pl.pallas_call(
        write_out,
        out_shape=tuple(jax.ShapeDtypeStruct(r.shape, r.dtype) for r in results),
        in_specs=[any_space] * 7,
        out_specs=(any_space,) * 7,
        scratch_shapes=[pltpu.VMEM(r.shape, r.dtype) for r in results] + [dma((7,)), dma((7,))],
    )(*results)


def solution(mesh):
    wide = P("ctx", "head")
    cache = P(("ctx", "head"), None)
    return jax.shard_map(
        on_device,
        mesh=mesh,
        in_specs=(wide, wide, cache, cache, wide, wide, wide, wide, P("head", "ctx"), P()),
        out_specs=(wide, cache, cache, wide, wide, wide, P("head", "ctx")),
        check_vma=False,
    )
```

```python
import jax
import jax.numpy as jnp
from jax import lax
from jax.experimental import pallas as pl
from jax.experimental.pallas import tpu as pltpu
from jax.sharding import PartitionSpec as P

ATTENDER_NUMBER = 24
KV_HEADS = 8
DH = 128
PER_GROUP = ATTENDER_NUMBER // KV_HEADS
ROWS = 512
TILE = 256
TILES = ROWS // TILE
DOC_BLOCKS = 4
STRIP = 128
X_RING = 4
SCALING = DH ** (-0.5)
EXPONENT_SCALE = SCALING * 1.4426950408889634
MESH = pl.DeviceIdType.MESH
BF16 = jnp.bfloat16
F32 = jnp.float32
STATE_ROWS = PER_GROUP * DH + 8


def matmul(a, b):
    return lax.dot_general(a, b, (((1,), (0,)), ((), ())), preferred_element_type=F32)


def matmul_nt(a, b):
    return lax.dot_general(a, b, (((1,), (1,)), ((), ())), preferred_element_type=F32)


def matmul_tn(a, b):
    return lax.dot_general(a, b, (((0,), (0,)), ((), ())), preferred_element_type=F32)


def exact_pieces(x):
    high = x.astype(BF16)
    rest = x - high.astype(F32)
    middle = rest.astype(BF16)
    low = (rest - middle.astype(F32)).astype(BF16)
    return jnp.concatenate([high, middle, low], axis=0)


def triangle_sum(x, triangle):
    parts = matmul(exact_pieces(x), triangle)
    return parts[0:16] + parts[16:32] + parts[32:48]


def body(
    n_ctx, n_head,
    cq, cg, ck, cv, rq_in, rk_in, rv_in, rg_in, ld, offs,
    gq_out, gk, gv, oq_out, ok_out, ov_out, dg,
    rq, rk, rv, rg, gq, oq, ok, ov, in_sem, tile_sem, out_sem,
    kvs, kvb, kv_thru, own_f, own_b, got_f, got_b, thru, part, half, back, grad_thru, home, wait_sum, final, landed, tot_x, tot_z,
    qs, os, kt, score, dprob, tops, prob_t, dscore_t,
    start_row, cum_row, cum_col, last_w, first_w, qf, kf, vf, pad16,
    head_s, head_r, kv_s, kv_r, st_s, st_r, gr_s, gr_r, fin_s, fin_r, tx_s, tx_r, tz_s, tz_r, ready,
):
    c = lax.axis_index("ctx")
    g = lax.axis_index("head")
    z_ring = n_ctx // X_RING
    slot_rows = ROWS // n_head

    def ctx_at(offset):
        return lax.rem(c + (offset + n_ctx), n_ctx)

    def head_at(offset):
        return lax.rem(g + offset, n_head)

    x = lax.rem(c, X_RING)
    z = c // X_RING

    def x_peer(offset):
        return z * X_RING + lax.rem(x + offset, X_RING)

    def z_peer(offset):
        return lax.rem(z + (offset + z_ring), z_ring) * X_RING + x

    def send(src, dst, send_sem, recv_sem, device):
        return pltpu.make_async_remote_copy(
            src_ref=src, dst_ref=dst, send_sem=send_sem, recv_sem=recv_sem,
            device_id=device, device_id_type=MESH,
        )

    def has(offset):
        if offset > 0:
            return c < n_ctx - offset
        return c >= -offset

    def z_has(offset):
        if offset > 0:
            return z < z_ring - offset
        return z >= -offset

    def start(transfer):
        pl.when(transfer[1])(lambda: transfer[0].start())

    def receive(transfer):
        pl.when(transfer[2])(lambda: transfer[0].wait_recv())

    def sent(transfer):
        pl.when(transfer[1])(lambda: transfer[0].wait_send())

    def clear(condition, ref):
        @pl.when(condition)
        def _():
            ref[...] = jnp.zeros(ref.shape, ref.dtype)

    barrier = pltpu.get_barrier_semaphore()
    greetings = n_head - 1 + X_RING - 1
    for k in range(1, n_head):
        pl.semaphore_signal(barrier, inc=1, device_id=(c, head_at(k)), device_id_type=MESH)
    for k in range(1, X_RING):
        pl.semaphore_signal(barrier, inc=1, device_id=(x_peer(k), g), device_id_type=MESH)
    for k in (1, -1, 3, -3):
        @pl.when(has(k))
        def _():
            pl.semaphore_signal(barrier, inc=1, device_id=(ctx_at(k), g), device_id_type=MESH)

        greetings = greetings + has(k).astype(jnp.int32)
    for k in (1, -1):
        if z_ring > 1:
            @pl.when(z_has(k))
            def _():
                pl.semaphore_signal(barrier, inc=1, device_id=(z_peer(k), g), device_id_type=MESH)

            greetings = greetings + z_has(k).astype(jnp.int32)

    def ready_round(r):
        if r < z_ring - 1:
            if r > 1:
                pl.when(z >= r)(lambda: pl.semaphore_wait(ready.at[r - 1], 1))

            @pl.when((z >= r) & (z < z_ring - 1))
            def _():
                pl.semaphore_signal(
                    ready.at[r], inc=1, device_id=(z_peer(1), g), device_id_type=MESH
                )

    loads = [
        pltpu.make_async_copy(source, held, in_sem.at[n])
        for n, (source, held) in enumerate(((rq_in, rq), (rk_in, rk), (rv_in, rv), (rg_in, rg)))
    ]
    for i in range(TILES):
        for h in range(PER_GROUP):
            rows = pl.ds((i * PER_GROUP + h) * TILE, TILE)
            block = (pl.ds(i * TILE, TILE), pl.ds(h * DH, DH))
            n = 2 * (i * PER_GROUP + h)
            loads.append(pltpu.make_async_copy(cq.at[block], qs.at[rows, :], tile_sem.at[n]))
            loads.append(pltpu.make_async_copy(cg.at[block], os.at[rows, :], tile_sem.at[n + 1]))
    for load in loads:
        load.start()

    for d in (1, 2, 3):
        clear(c < d, kvb.at[d])
        clear(c < d, got_f.at[d - 1])
        clear(c >= n_ctx - d, got_b.at[d - 1])
    clear((c == 0) | (c == n_ctx - 1), half.at[0])
    clear(c < 3, half.at[1])
    clear(c != n_ctx - 2, half.at[2])
    clear(c >= n_ctx - 1, back.at[0])
    clear(c >= n_ctx - 3, back.at[1])

    kvs[0] = ck[...]
    kvs[1] = cv[...]
    base = (c * ROWS).astype(F32)
    offsets = offs[...].astype(F32)
    pos_col = lax.broadcasted_iota(jnp.int32, (ROWS, 1), 0).astype(F32)
    begun = jnp.where(offsets <= pos_col + base, offsets, 0.0)
    start_col = jnp.max(begun, axis=1, keepdims=True) - base
    start_row[...] = jnp.broadcast_to(start_col, (ROWS, DH)).T[0:8]
    start_last = start_col[ROWS - 1 : ROWS, :]
    row_at = lax.broadcasted_iota(jnp.int32, (ROWS, ROWS), 0)
    col_at = lax.broadcasted_iota(jnp.int32, (ROWS, ROWS), 1)

    pad16[...] = jnp.zeros_like(pad16)
    pad16[0:PER_GROUP, :] = ld[...]
    cum = triangle_sum(pad16[...], (row_at <= col_at).astype(F32).astype(BF16))
    cum_row[...] = cum
    cum_t = jnp.concatenate([cum, jnp.zeros((DH - 16, ROWS), F32)], axis=0).T
    pl.semaphore_wait(barrier, greetings)

    head_copies = []
    for k in range(1, n_head):
        to = head_at(k)
        copy = send(
            kvs.at[:, :, pl.ds(pl.multiple_of(to * DH, DH), DH)],
            kvb.at[0, :, pl.ds(pl.multiple_of(g * slot_rows, slot_rows), slot_rows), :],
            head_s.at[k], head_r.at[k], (c, to),
        )
        copy.start()
        head_copies.append(copy)
    kvb[0, :, pl.ds(pl.multiple_of(g * slot_rows, slot_rows), slot_rows), :] = kvs[
        :, :, pl.ds(pl.multiple_of(g * DH, DH), DH)
    ]

    ready_round(1)

    for load in loads[:4]:
        load.wait()
    carry_rows = []
    for h in range(PER_GROUP):
        lanes = slice(h * DH, (h + 1) * DH)
        col = cum_t[:, h : h + 1]
        final_cum = col[ROWS - 1 : ROWS, :]
        last = jnp.where(pos_col >= start_last, jnp.exp(final_cum - col), 0.0)
        first = jnp.where(start_col < 0.0, jnp.exp(col), 0.0) * SCALING
        cum_col[h] = jnp.broadcast_to(col, (ROWS, DH))
        last = jnp.broadcast_to(last, (ROWS, DH))
        first = jnp.broadcast_to(first, (ROWS, DH))
        last_w[h] = last
        first_w[h] = first
        keys_w = (last * rk[:, lanes].astype(F32)).astype(BF16)
        queries_w = (first * rq[:, lanes].astype(F32)).astype(BF16)
        own_f[h * DH : (h + 1) * DH, :] = matmul_tn(keys_w, rv[:, lanes])
        own_b[h * DH : (h + 1) * DH, :] = matmul_tn(queries_w, rg[:, lanes])
        carry = jnp.where(start_last < 0.0, jnp.exp(final_cum), 0.0)
        carry_rows.append(jnp.broadcast_to(carry, (8, DH)))
    which = lax.broadcasted_iota(jnp.int32, (8, DH), 0)
    carries = jnp.zeros((8, DH), F32)
    for h in range(PER_GROUP):
        carries = jnp.where(which == h, carry_rows[h], carries)
    own_f[PER_GROUP * DH :, :] = carries
    own_b[PER_GROUP * DH :, :] = carries

    for copy in head_copies:
        copy.wait_recv()
    up, down = (ctx_at(1), g), (ctx_at(-1), g)
    far_up, far_down = (ctx_at(3), g), (ctx_at(-3), g)

    def transfer(sems, n, src, dst, device, sends, receives):
        return send(src, dst, sems[0].at[n], sems[1].at[n], device), sends, receives

    kv_sems, st_sems, gr_sems = (kv_s, kv_r), (st_s, st_r), (gr_s, gr_r)
    over = (ctx_at(4), g)
    inner, outer = (c >= 1) & (x > 0), x == 0
    upper, lower = pl.ds(0, TILE), pl.ds(TILE, TILE)
    kv_copies = [
        transfer(kv_sems, 0, kvb.at[0, 0], kvb.at[1, 0], up, has(1) & (x < 3), inner),
        transfer(kv_sems, 1, kvb.at[0, 1], kvb.at[3, 1], far_up, has(3), has(-3)),
        transfer(kv_sems, 2, kvb.at[0, 1], kvb.at[1, 1], up, has(1) & (x < 3), inner),
        transfer(kv_sems, 3, kvb.at[0, 0], kvb.at[3, 0], far_up, has(3), has(-3)),
        transfer(kv_sems, 4, kvb.at[1, 0, upper], kvb.at[2, 0, upper], up, has(1) & inner, has(-2)),
        transfer(
            kv_sems, 5, kvb.at[3, 1], kvb.at[2, 1], down, has(-3), (c >= 2) & (c < n_ctx - 1)
        ),
        transfer(kv_sems, 6, kvb.at[1, 1], kvb.at[2, 1], up, c == n_ctx - 2, c == n_ctx - 1),
        transfer(
            kv_sems, 7, kvb.at[0, 0, upper], kv_thru.at[0, upper], far_down,
            (x == 3) & has(1), outer & has(4),
        ),
        transfer(kv_sems, 8, kvb.at[0, 1], kv_thru.at[1], far_down, (x == 3) & has(1), outer & has(4)),
        transfer(
            kv_sems, 9, kv_thru.at[0, upper], kvb.at[1, 0, upper], over,
            outer & has(4), outer & has(-4),
        ),
        transfer(kv_sems, 10, kv_thru.at[1], kvb.at[1, 1], over, outer & has(4), outer & has(-4)),
        transfer(
            kv_sems, 4, kvb.at[1, 0, upper], kvb.at[2, 0, upper], up,
            outer & has(1) & has(-4), has(-2),
        ),
        transfer(kv_sems, 11, kvb.at[1, 0, lower], kvb.at[2, 0, lower], up, has(1) & inner, has(-2)),
        transfer(
            kv_sems, 12, kvb.at[0, 0, lower], kv_thru.at[0, lower], far_down,
            (x == 3) & has(1), outer & has(4),
        ),
        transfer(
            kv_sems, 13, kv_thru.at[0, lower], kvb.at[1, 0, lower], over,
            outer & has(4), outer & has(-4),
        ),
        transfer(
            kv_sems, 11, kvb.at[1, 0, lower], kvb.at[2, 0, lower], up,
            outer & has(1) & has(-4), has(-2),
        ),
    ]
    state_copies = [
        transfer(st_sems, 0, own_f, got_f.at[0], up, has(1) & (x < 3), has(-1) & (x > 0)),
        transfer(st_sems, 1, own_b, got_b.at[0], down, has(-1), has(1)),
        transfer(st_sems, 2, own_f, got_f.at[2], far_up, has(3) & (x < 3), has(-3) & (x != 2)),
        transfer(st_sems, 3, own_b, got_b.at[2], far_down, has(-3), has(3)),
        transfer(st_sems, 4, got_f.at[0], got_f.at[1], up, has(1) & has(-1), has(-2)),
        transfer(st_sems, 5, got_b.at[0], got_b.at[1], down, has(1) & has(-1), has(2)),
        transfer(st_sems, 6, own_f, thru, far_down, (x == 3) & has(1), (x == 0) & has(4)),
        transfer(st_sems, 7, own_f, thru, down, (x == 3) & has(3), (x == 2) & has(4)),
        transfer(st_sems, 8, thru, got_f.at[0], over, (x == 0) & has(4), (x == 0) & has(-4)),
        transfer(st_sems, 9, thru, got_f.at[2], over, (x == 2) & has(4), (x == 2) & has(-4)),
    ]
    for n in (7, 13, 0, 1, 8, 2, 3):
        start(kv_copies[n])
    ready_round(2)

    for load in loads[4:]:
        load.wait()

    tile_row = lax.broadcasted_iota(jnp.int32, (TILE, TILE), 0)
    tile_col = lax.broadcasted_iota(jnp.int32, (TILE, TILE), 1)
    tile_pos = tile_row.astype(F32)
    causal = tile_row <= tile_col

    def retention_head(h, nothing):
        lanes = pl.ds(pl.multiple_of(h * DH, DH), DH)
        for ti in range(TILES):
            t = slice(ti * TILE, (ti + 1) * TILE)
            rq_t = rq[t, lanes]
            rg_t = rg[t, lanes]
            cum_t_row = cum_row[pl.ds(h, 1), t]
            query_t = jnp.zeros((DH, TILE), F32)
            for si in range(ti + 1):
                s = slice(si * TILE, (si + 1) * TILE)
                rk_s = rk[s, lanes]
                allowed = tile_pos >= start_row[0:1, t] - float(si * TILE)
                if si == ti:
                    allowed = allowed & causal
                gap = jnp.minimum(cum_t_row - cum_col[h, s, 0:1], 0.0)
                within = jnp.where(allowed, jnp.exp(gap) * SCALING, 0.0)
                grad_w = (within * matmul_nt(rv[s, lanes], rg_t)).astype(BF16)
                score_w = (within * matmul_nt(rk_s, rq_t)).astype(BF16)
                query_t = query_t + matmul_tn(rk_s, grad_w)
                key_term = matmul(grad_w, rq_t)
                value_term = matmul(score_w, rg_t)
                if si == ti:
                    kf[h, s, :] = key_term
                    vf[h, s, :] = value_term
                else:
                    kf[h, s, :] = kf[h, s, :] + key_term
                    vf[h, s, :] = vf[h, s, :] + value_term
            qf[h, t, :] = query_t.T

        return nothing

    lax.fori_loop(0, PER_GROUP, retention_head, 0)

    def tile_strips(i):
        strips = []
        for d in range(DOC_BLOCKS):
            first, stop = (0, (i + 1) * TILE) if d == 0 else (0, ROWS)
            if d == DOC_BLOCKS - 1:
                first = i * TILE
            strips += [(d, at) for at in range(first, stop, STRIP)]
        return strips

    def tile_columns(h, i):
        return pl.ds(pl.multiple_of(i * (PER_GROUP * TILE) + h * TILE, TILE), TILE)

    def scores_of_block(block):
        def one_head(h, nothing):
            for i in range(TILES):
                at_tile = h * TILES + i
                cols = tile_columns(h, i)
                query = qs[cols, :]
                upstream = os[cols, :]
                start_t = start_row[0:1, i * TILE : (i + 1) * TILE]
                top = jnp.full((8, TILE), -1e30, F32) if block == 0 else tops[at_tile]
                for n, (d, at_s) in enumerate(tile_strips(i)):
                    if d != block:
                        continue
                    s = slice(at_s, at_s + STRIP)
                    at = slice(n * STRIP, (n + 1) * STRIP)
                    raw = matmul_nt(kvb[d, 0, s, :], query) * EXPONENT_SCALE
                    allowed = strip_pos >= start_t + float(d * ROWS - at_s)
                    if d == 0 and at_s >= i * TILE:
                        allowed = allowed & (strip_row + (at_s - i * TILE) <= strip_col)
                    raw = jnp.where(allowed, raw, -1e30)
                    score[at_tile, at, :] = raw
                    top = jnp.maximum(top, jnp.max(raw.reshape(STRIP // 8, 8, TILE), axis=0))
                    dprob[at_tile, at, :] = matmul_nt(kvb[d, 1, s, :], upstream)
                tops[at_tile] = top
            return nothing

        lax.fori_loop(0, PER_GROUP, one_head, 0)

    strip_row = lax.broadcasted_iota(jnp.int32, (STRIP, TILE), 0)
    strip_col = lax.broadcasted_iota(jnp.int32, (STRIP, TILE), 1)
    strip_pos = strip_row.astype(F32)

    receive(kv_copies[7])
    start(kv_copies[9])
    receive(kv_copies[13])
    start(kv_copies[14])
    receive(kv_copies[0])
    start(kv_copies[4])
    start(kv_copies[12])
    receive(kv_copies[1])
    start(kv_copies[5])
    for n in (6, 7, 1, 0, 3, 2):
        start(state_copies[n])
    scores_of_block(0)
    receive(kv_copies[9])
    start(kv_copies[11])
    receive(kv_copies[8])
    start(kv_copies[10])
    receive(kv_copies[14])
    start(kv_copies[15])
    receive(kv_copies[2])
    start(kv_copies[6])
    receive(kv_copies[3])
    ready_round(3)
    scores_of_block(3)
    receive(kv_copies[10])
    scores_of_block(1)
    for n in (6, 7):
        receive(state_copies[n])
        start(state_copies[n + 2])
    for d in (0, 1, 3):
        kt[d] = kvb[d, 0].astype(F32).T.astype(BF16)
    for n in (4, 12, 5, 6):
        receive(kv_copies[n])
    kt[2] = kvb[2, 0].astype(F32).T.astype(BF16)
    receive(state_copies[1])
    start(state_copies[5])
    scores_of_block(2)
    receive(state_copies[0])
    receive(state_copies[8])
    start(state_copies[4])

    def attention_head(h, nothing):
        for i in range(TILES):
            at_tile = h * TILES + i
            cols = tile_columns(h, i)
            strips = tile_strips(i)
            top = jnp.max(tops[at_tile], axis=0, keepdims=True)
            total = jnp.zeros((8, TILE), F32)
            for n in range(len(strips)):
                at = slice(n * STRIP, (n + 1) * STRIP)
                term = jnp.exp2(score[at_tile, at, :] - top)
                score[at_tile, at, :] = term
                total = total + jnp.sum(term.reshape(STRIP // 8, 8, TILE), axis=0)
            inverse = 1.0 / jnp.sum(total, axis=0, keepdims=True)
            row_dot = jnp.zeros((8, TILE), F32)
            for n, (d, at_s) in enumerate(strips):
                s = slice(at_s, at_s + STRIP)
                at = slice(n * STRIP, (n + 1) * STRIP)
                weights = score[at_tile, at, :] * inverse
                weights_b = weights.astype(BF16)
                prob_t[d, s, cols] = weights_b
                products = weights_b.astype(F32) * dprob[at_tile, at, :]
                row_dot = row_dot + jnp.sum(products.reshape(STRIP // 8, 8, TILE), axis=0)
            row_dot = jnp.sum(row_dot, axis=0, keepdims=True)
            query_t = jnp.zeros((DH, TILE), F32)
            for n, (d, at_s) in enumerate(strips):
                s = slice(at_s, at_s + STRIP)
                at = slice(n * STRIP, (n + 1) * STRIP)
                gaps = dprob[at_tile, at, :] - row_dot
                dscores_b = ((score[at_tile, at, :] * inverse) * gaps).astype(BF16)
                dscore_t[d, s, cols] = dscores_b
            for d in range(DOC_BLOCKS):
                first, stop = (0, (i + 1) * TILE) if d == 0 else (0, ROWS)
                if d == DOC_BLOCKS - 1:
                    first = i * TILE
                query_t = query_t + matmul(kt[d, :, first:stop], dscore_t[d, first:stop, cols])
            gq[i * TILE : (i + 1) * TILE, pl.ds(pl.multiple_of(h * DH, DH), DH)] = (
                query_t.T * SCALING
            ).astype(BF16)

        @pl.when(h == 0)
        def _():
            ready_round(4)

        @pl.when(h == 1)
        def _():
            ready_round(5)

        return nothing

    lax.fori_loop(0, PER_GROUP, attention_head, 0)

    stores = [pltpu.make_async_copy(gq, gq_out, out_sem.at[0])]
    stores[0].start()

    width = PER_GROUP * TILE

    def partial_at(d, j):
        cols = slice(0, TILES * width)
        if d == 0:
            cols = slice(j * width, TILES * width)
        if d == 3:
            cols = slice(0, (j + 1) * width)
        return slice(j * TILE, (j + 1) * TILE), cols

    middle_device = has(1) & has(-1)
    grad_copies = [
        transfer(gr_sems, 0, part.at[1, 0], half.at[0], down, has(-2), middle_device),
        transfer(gr_sems, 1, part.at[1, 1], half.at[1], up, has(-2) & has(1), has(-3)),
        transfer(gr_sems, 2, part.at[1, 1], half.at[2], down, c == n_ctx - 1, c == n_ctx - 2),
        transfer(gr_sems, 3, part.at[2, 0], back.at[1, 0], far_down, has(-3), has(3)),
        transfer(
            gr_sems, 4, part.at[0, 1], back.at[0, 1], down, has(-1) & (x > 0), has(1) & (x < 3)
        ),
        transfer(gr_sems, 5, part.at[2, 1], back.at[1, 1], far_down, has(-3), has(3)),
        transfer(gr_sems, 6, part.at[0, 0], back.at[0, 0], down, has(-1), has(1)),
        transfer(gr_sems, 7, part.at[0, 1], grad_thru, far_up, (x == 0) & has(-4), (x == 3) & has(-4)),
        transfer(
            gr_sems, 8, grad_thru, back.at[0, 1], (ctx_at(-4), g), (x == 3) & has(-4), (x == 3) & has(4)
        ),
    ]

    def key_grad(d, out, at):
        for j in range(TILES):
            s, cols = partial_at(d, j)
            value = matmul(dscore_t[d, s, cols], qs[cols, :]) * SCALING
            out[at + (s,)] = value.astype(out.dtype)

    def value_grad(d, out, at):
        for j in range(TILES):
            s, cols = partial_at(d, j)
            value = matmul(prob_t[d, s, cols], os[cols, :])
            out[at + (s,)] = value.astype(out.dtype)

    key_grad(2, part, (1, 0))
    start(grad_copies[0])
    value_grad(2, part, (1, 1))
    start(grad_copies[1])
    start(grad_copies[2])
    key_grad(3, part, (2, 0))
    start(grad_copies[3])
    value_grad(1, wait_sum, (0,))

    receive(grad_copies[2])

    part[0, 1] = (wait_sum[0] + half[2].astype(F32)).astype(BF16)
    start(grad_copies[4])
    start(grad_copies[7])
    value_grad(3, wait_sum, (1,))
    key_grad(1, wait_sum, (2,))
    key_grad(0, home, (0,))
    value_grad(0, home, (1,))
    ready_round(6)

    for n in (2, 3, 4, 5, 9):
        receive(state_copies[n])
    sums = jnp.zeros((ROWS, DH), F32)
    lane_at = lax.broadcasted_iota(jnp.int32, (ROWS, DH), 1)
    for h in range(PER_GROUP):
        lanes = slice(h * DH, (h + 1) * DH)
        block = slice(h * DH, (h + 1) * DH)
        carry_at = slice(PER_GROUP * DH + h, PER_GROUP * DH + h + 1)

        def chained(got):
            inner = got[1, block, :] + got[1, carry_at, :] * got[2, block, :]
            return (got[0, block, :] + got[0, carry_at, :] * inner).astype(BF16)

        state_b = jnp.where(c > 0, chained(got_f), jnp.zeros((DH, DH), BF16))
        later_b = jnp.where(c < n_ctx - 1, chained(got_b), jnp.zeros((DH, DH), BF16))
        last = last_w[h]
        query_f = qf[h] + first_w[h] * matmul_nt(rg[:, lanes], state_b)
        key_f = kf[h] + last * matmul_nt(rv[:, lanes], later_b)
        value_f = vf[h] + last * matmul(rk[:, lanes], later_b)
        oq[:, lanes] = query_f.astype(BF16)
        ok[:, lanes] = key_f.astype(BF16)
        ov[:, lanes] = value_f.astype(BF16)
        residue = jnp.sum(rq[:, lanes].astype(F32) * query_f, axis=1, keepdims=True) - jnp.sum(
            rk[:, lanes].astype(F32) * key_f, axis=1, keepdims=True
        )
        sums = jnp.where(lane_at == h, residue, sums)
    for n, (held, target) in enumerate(((oq, oq_out), (ok, ok_out), (ov, ov_out))):
        stores.append(pltpu.make_async_copy(held, target, out_sem.at[n + 1]))
        stores[-1].start()
    suffix = triangle_sum(sums.T[0:16], (row_at >= col_at).astype(F32).astype(BF16))
    cum_row[...] = suffix
    tot_x[0] = jnp.broadcast_to(suffix[0:8, 0:1], (8, DH))
    x_copies = [
        send(tot_x.at[0], tot_x.at[k], tx_s.at[k], tx_r.at[k], (x_peer(k), g))
        for k in range(1, X_RING)
    ]
    for copy in x_copies:
        copy.start()

    receive(grad_copies[7])
    start(grad_copies[8])
    receive(grad_copies[1])
    part[2, 1] = (wait_sum[1] + half[1].astype(F32)).astype(BF16)
    start(grad_copies[5])
    receive(grad_copies[0])
    part[0, 0] = (wait_sum[2] + half[0].astype(F32)).astype(BF16)
    start(grad_copies[6])

    for copy in x_copies:
        copy.wait_recv()
    row_total = tot_x[0]
    tail = jnp.zeros((8, DH), F32)
    for k in range(1, X_RING):
        row_total = row_total + tot_x[k]
        tail = tail + jnp.where(lax.rem(x - k + X_RING, X_RING) > x, tot_x[k], 0.0)
    tot_z[0] = row_total
    z_copies = [
        transfer((tz_s, tz_r), k, tot_z.at[0], tot_z.at[k], (z_peer(-k), g), z_has(-k), z_has(k))
        for k in range(1, z_ring)
    ]
    if z_ring > 2:
        pl.when(z >= z_ring - 1)(lambda: pl.semaphore_wait(ready.at[z_ring - 2], 1))
    for copy in z_copies:
        start(copy)

    for n in (3, 4, 5, 6, 8):
        receive(grad_copies[n])
    for m in range(2):
        total = home[m] + back[0, m].astype(F32) + back[1, m].astype(F32)
        final[m] = total.astype(BF16)
    final_copies = []
    for k in range(1, n_head):
        to = head_at(k)
        copy = send(
            final.at[:, pl.ds(pl.multiple_of(to * slot_rows, slot_rows), slot_rows), :],
            landed.at[:, :, pl.ds(pl.multiple_of(g * DH, DH), DH)],
            fin_s.at[k], fin_r.at[k], (c, to),
        )
        copy.start()
        final_copies.append(copy)
    landed[:, :, pl.ds(pl.multiple_of(g * DH, DH), DH)] = final[
        :, pl.ds(pl.multiple_of(g * slot_rows, slot_rows), slot_rows), :
    ]

    for copy in z_copies:
        receive(copy)
    for k in range(1, z_ring):
        tail = tail + jnp.where(z_has(k), tot_z[k], 0.0)
    dg[...] = (cum_row[0:8, :] + tail[:, 0:1])[0:PER_GROUP]

    for copy in final_copies:
        copy.wait_recv()
    for m, target in enumerate((gk, gv)):
        stores.append(pltpu.make_async_copy(landed.at[m], target, out_sem.at[m + 4]))
        stores[-1].start()
    for store in stores:
        store.wait()
    for copy in head_copies + x_copies + final_copies:
        copy.wait_send()
    for copy in kv_copies + state_copies + grad_copies + z_copies:
        sent(copy)


def write_out(*refs):
    count = 7
    sources, targets, held = refs[:count], refs[count : 2 * count], refs[2 * count : 3 * count]
    sem_in, sem_out = refs[3 * count :]
    loads = [pltpu.make_async_copy(sources[n], held[n], sem_in.at[n]) for n in range(count)]
    stores = [pltpu.make_async_copy(held[n], targets[n], sem_out.at[n]) for n in range(count)]
    for load in loads:
        load.start()
    for load, store in zip(loads, stores):
        load.wait()
        store.start()
    for store in stores:
        store.wait()


def on_device(
    cross_query, cross_grad, cache_keys, cache_values, retention_query, retention_key,
    retention_value, retention_grad, log_decay, doc_offsets,
):
    n_ctx = lax.axis_size("ctx")
    n_head = lax.axis_size("head")
    wide = jax.ShapeDtypeStruct(cross_query.shape, BF16)
    cache = jax.ShapeDtypeStruct(cache_keys.shape, BF16)
    vmem = pl.BlockSpec(memory_space=pltpu.VMEM)
    slot_rows, all_heads = cache_keys.shape
    dma = pltpu.SemaphoreType.DMA
    any_space = pl.BlockSpec(memory_space=pl.ANY)
    heads_wide = pltpu.VMEM((PER_GROUP, ROWS, DH), F32)
    results = pl.pallas_call(
        lambda *refs: body(n_ctx, n_head, *refs),
        out_shape=(
            wide, cache, cache, wide, wide, wide, jax.ShapeDtypeStruct(log_decay.shape, F32),
        ),
        in_specs=[any_space] * 2 + [vmem] * 2 + [any_space] * 4 + [vmem] * 2,
        out_specs=(any_space,) * 6 + (vmem,),
        scratch_shapes=[
            *[pltpu.VMEM(cross_query.shape, BF16)] * 8,
            dma((4,)), dma((2 * PER_GROUP * TILES,)), dma((6,)),
            pltpu.VMEM((2, slot_rows, all_heads), BF16),
            pltpu.VMEM((4, 2, ROWS, DH), BF16),
            pltpu.VMEM((2, ROWS, DH), BF16),
            pltpu.VMEM((STATE_ROWS, DH), F32),
            pltpu.VMEM((STATE_ROWS, DH), F32),
            pltpu.VMEM((3, STATE_ROWS, DH), F32),
            pltpu.VMEM((3, STATE_ROWS, DH), F32),
            pltpu.VMEM((STATE_ROWS, DH), F32),
            pltpu.VMEM((3, 2, ROWS, DH), BF16),
            pltpu.VMEM((3, ROWS, DH), BF16),
            pltpu.VMEM((2, 2, ROWS, DH), BF16),
            pltpu.VMEM((ROWS, DH), BF16),
            pltpu.VMEM((2, ROWS, DH), F32),
            pltpu.VMEM((3, ROWS, DH), F32),
            pltpu.VMEM((2, ROWS, DH), BF16),
            pltpu.VMEM((2, slot_rows, all_heads), BF16),
            pltpu.VMEM((X_RING, 8, DH), F32),
            pltpu.VMEM((max(n_ctx // X_RING, 1), 8, DH), F32),
            pltpu.VMEM((PER_GROUP * ROWS, DH), BF16),
            pltpu.VMEM((PER_GROUP * ROWS, DH), BF16),
            pltpu.VMEM((4, DH, ROWS), BF16),
            pltpu.VMEM((PER_GROUP * TILES, 7 * TILE, TILE), F32),
            pltpu.VMEM((PER_GROUP * TILES, 7 * TILE, TILE), F32),
            pltpu.VMEM((PER_GROUP * TILES, 8, TILE), F32),
            pltpu.VMEM((4, ROWS, PER_GROUP * ROWS), BF16),
            pltpu.VMEM((4, ROWS, PER_GROUP * ROWS), BF16),
            pltpu.VMEM((8, ROWS), F32),
            pltpu.VMEM((16, ROWS), F32),
            heads_wide,
            heads_wide,
            heads_wide,
            heads_wide,
            heads_wide,
            heads_wide,
            pltpu.VMEM((16, ROWS), F32),
            dma((8,)), dma((8,)), dma((14,)), dma((14,)), dma((10,)), dma((10,)), dma((9,)), dma((9,)),
            dma((8,)), dma((8,)), dma((4,)), dma((4,)), dma((8,)), dma((8,)),
            pltpu.SemaphoreType.REGULAR((8,)),
        ],
        compiler_params=pltpu.CompilerParams(
            collective_id=0, has_side_effects=True, vmem_limit_bytes=56 * 1024 * 1024
        ),
    )(
        cross_query, cross_grad, cache_keys, cache_values, retention_query, retention_key,
        retention_value, retention_grad, log_decay, doc_offsets.reshape(1, -1),
    )
    return pl.pallas_call(
        write_out,
        out_shape=tuple(jax.ShapeDtypeStruct(r.shape, r.dtype) for r in results),
        in_specs=[any_space] * 7,
        out_specs=(any_space,) * 7,
        scratch_shapes=[pltpu.VMEM(r.shape, r.dtype) for r in results] + [dma((7,)), dma((7,))],
    )(*results)


def solution(mesh):
    wide = P("ctx", "head")
    cache = P(("ctx", "head"), None)
    return jax.shard_map(
        on_device,
        mesh=mesh,
        in_specs=(wide, wide, cache, cache, wide, wide, wide, wide, P("head", "ctx"), P()),
        out_specs=(wide, cache, cache, wide, wide, wide, P("head", "ctx")),
        check_vma=False,
    )
```

```python
import jax
import jax.numpy as jnp
from jax import lax
from jax.experimental import pallas as pl
from jax.experimental.pallas import tpu as pltpu
from jax.sharding import PartitionSpec as P

ATTENDER_NUMBER = 24
KV_HEADS = 8
DH = 128
PER_GROUP = ATTENDER_NUMBER // KV_HEADS
ROWS = 512
TILE = 256
TILES = ROWS // TILE
DOC_BLOCKS = 4
STRIP = 128
X_RING = 4
SCALING = DH ** (-0.5)
EXPONENT_SCALE = SCALING * 1.4426950408889634
MESH = pl.DeviceIdType.MESH
BF16 = jnp.bfloat16
F32 = jnp.float32
STATE_ROWS = PER_GROUP * DH + 8


def matmul(a, b):
    return lax.dot_general(a, b, (((1,), (0,)), ((), ())), preferred_element_type=F32)


def matmul_nt(a, b):
    return lax.dot_general(a, b, (((1,), (1,)), ((), ())), preferred_element_type=F32)


def matmul_tn(a, b):
    return lax.dot_general(a, b, (((0,), (0,)), ((), ())), preferred_element_type=F32)


def exact_pieces(x):
    high = x.astype(BF16)
    rest = x - high.astype(F32)
    middle = rest.astype(BF16)
    low = (rest - middle.astype(F32)).astype(BF16)
    return jnp.concatenate([high, middle, low], axis=0)


def triangle_sum(x, triangle):
    parts = matmul(exact_pieces(x), triangle)
    return parts[0:16] + parts[16:32] + parts[32:48]


def body(
    n_ctx, n_head,
    cq, cg, ck, cv, rq_in, rk_in, rv_in, rg_in, ld, offs,
    gq_out, gk, gv, oq_out, ok_out, ov_out, dg,
    rq, rk, rv, rg, gq, oq, ok, ov, in_sem, tile_sem, out_sem,
    kvs, kvb, kv_thru, own_f, own_b, got_f, got_b, thru, part, half, back, grad_thru, home, wait_sum, final, landed, tot_x, tot_z,
    qs, os, kt, score, dprob, tops, prob_t, dscore_t,
    start_row, cum_row, cum_col, last_w, first_w, qf, kf, vf, pad16,
    head_s, head_r, kv_s, kv_r, st_s, st_r, gr_s, gr_r, fin_s, fin_r, tx_s, tx_r, tz_s, tz_r, ready,
):
    c = lax.axis_index("ctx")
    g = lax.axis_index("head")
    z_ring = n_ctx // X_RING
    slot_rows = ROWS // n_head

    def ctx_at(offset):
        return lax.rem(c + (offset + n_ctx), n_ctx)

    def head_at(offset):
        return lax.rem(g + offset, n_head)

    x = lax.rem(c, X_RING)
    z = c // X_RING

    def x_peer(offset):
        return z * X_RING + lax.rem(x + offset, X_RING)

    def z_peer(offset):
        return lax.rem(z + (offset + z_ring), z_ring) * X_RING + x

    def send(src, dst, send_sem, recv_sem, device):
        return pltpu.make_async_remote_copy(
            src_ref=src, dst_ref=dst, send_sem=send_sem, recv_sem=recv_sem,
            device_id=device, device_id_type=MESH,
        )

    def has(offset):
        if offset > 0:
            return c < n_ctx - offset
        return c >= -offset

    def z_has(offset):
        if offset > 0:
            return z < z_ring - offset
        return z >= -offset

    def start(transfer):
        pl.when(transfer[1])(lambda: transfer[0].start())

    def receive(transfer):
        pl.when(transfer[2])(lambda: transfer[0].wait_recv())

    def sent(transfer):
        pl.when(transfer[1])(lambda: transfer[0].wait_send())

    def clear(condition, ref):
        @pl.when(condition)
        def _():
            ref[...] = jnp.zeros(ref.shape, ref.dtype)

    barrier = pltpu.get_barrier_semaphore()
    greetings = n_head - 1 + X_RING - 1
    for k in range(1, n_head):
        pl.semaphore_signal(barrier, inc=1, device_id=(c, head_at(k)), device_id_type=MESH)
    for k in range(1, X_RING):
        pl.semaphore_signal(barrier, inc=1, device_id=(x_peer(k), g), device_id_type=MESH)
    for k in (1, -1, 3, -3):
        @pl.when(has(k))
        def _():
            pl.semaphore_signal(barrier, inc=1, device_id=(ctx_at(k), g), device_id_type=MESH)

        greetings = greetings + has(k).astype(jnp.int32)
    for k in (1, -1):
        if z_ring > 1:
            @pl.when(z_has(k))
            def _():
                pl.semaphore_signal(barrier, inc=1, device_id=(z_peer(k), g), device_id_type=MESH)

            greetings = greetings + z_has(k).astype(jnp.int32)

    def ready_round(r):
        if r < z_ring - 1:
            if r > 1:
                pl.when(z >= r)(lambda: pl.semaphore_wait(ready.at[r - 1], 1))

            @pl.when((z >= r) & (z < z_ring - 1))
            def _():
                pl.semaphore_signal(
                    ready.at[r], inc=1, device_id=(z_peer(1), g), device_id_type=MESH
                )

    loads = [
        pltpu.make_async_copy(source, held, in_sem.at[n])
        for n, (source, held) in enumerate(((rq_in, rq), (rk_in, rk), (rv_in, rv), (rg_in, rg)))
    ]
    for i in range(TILES):
        for h in range(PER_GROUP):
            rows = pl.ds((i * PER_GROUP + h) * TILE, TILE)
            block = (pl.ds(i * TILE, TILE), pl.ds(h * DH, DH))
            n = 2 * (i * PER_GROUP + h)
            loads.append(pltpu.make_async_copy(cq.at[block], qs.at[rows, :], tile_sem.at[n]))
            loads.append(pltpu.make_async_copy(cg.at[block], os.at[rows, :], tile_sem.at[n + 1]))
    for load in loads:
        load.start()

    for d in (1, 2, 3):
        clear(c < d, kvb.at[d])
        clear(c < d, got_f.at[d - 1])
        clear(c >= n_ctx - d, got_b.at[d - 1])
    clear((c == 0) | (c == n_ctx - 1), half.at[0])
    clear(c < 3, half.at[1])
    clear(c != n_ctx - 2, half.at[2])
    clear(c >= n_ctx - 1, back.at[0])
    clear(c >= n_ctx - 3, back.at[1])

    kvs[0] = ck[...]
    kvs[1] = cv[...]
    base = (c * ROWS).astype(F32)
    offsets = offs[...].astype(F32)
    pos_col = lax.broadcasted_iota(jnp.int32, (ROWS, 1), 0).astype(F32)
    begun = jnp.where(offsets <= pos_col + base, offsets, 0.0)
    start_col = jnp.max(begun, axis=1, keepdims=True) - base
    start_row[...] = jnp.broadcast_to(start_col, (ROWS, DH)).T[0:8]
    start_last = start_col[ROWS - 1 : ROWS, :]
    row_at = lax.broadcasted_iota(jnp.int32, (ROWS, ROWS), 0)
    col_at = lax.broadcasted_iota(jnp.int32, (ROWS, ROWS), 1)

    pad16[...] = jnp.zeros_like(pad16)
    pad16[0:PER_GROUP, :] = ld[...]
    cum = triangle_sum(pad16[...], (row_at <= col_at).astype(F32).astype(BF16))
    cum_row[...] = cum
    cum_t = jnp.concatenate([cum, jnp.zeros((DH - 16, ROWS), F32)], axis=0).T
    pl.semaphore_wait(barrier, greetings)

    head_copies = []
    for k in range(1, n_head):
        to = head_at(k)
        copy = send(
            kvs.at[:, :, pl.ds(pl.multiple_of(to * DH, DH), DH)],
            kvb.at[0, :, pl.ds(pl.multiple_of(g * slot_rows, slot_rows), slot_rows), :],
            head_s.at[k], head_r.at[k], (c, to),
        )
        copy.start()
        head_copies.append(copy)
    kvb[0, :, pl.ds(pl.multiple_of(g * slot_rows, slot_rows), slot_rows), :] = kvs[
        :, :, pl.ds(pl.multiple_of(g * DH, DH), DH)
    ]

    ready_round(1)

    for load in loads[:4]:
        load.wait()
    carry_rows = []
    for h in range(PER_GROUP):
        lanes = slice(h * DH, (h + 1) * DH)
        col = cum_t[:, h : h + 1]
        final_cum = col[ROWS - 1 : ROWS, :]
        last = jnp.where(pos_col >= start_last, jnp.exp(final_cum - col), 0.0)
        first = jnp.where(start_col < 0.0, jnp.exp(col), 0.0) * SCALING
        cum_col[h] = jnp.broadcast_to(col, (ROWS, DH))
        last = jnp.broadcast_to(last, (ROWS, DH))
        first = jnp.broadcast_to(first, (ROWS, DH))
        last_w[h] = last
        first_w[h] = first
        keys_w = (last * rk[:, lanes].astype(F32)).astype(BF16)
        queries_w = (first * rq[:, lanes].astype(F32)).astype(BF16)
        own_f[h * DH : (h + 1) * DH, :] = matmul_tn(keys_w, rv[:, lanes])
        own_b[h * DH : (h + 1) * DH, :] = matmul_tn(queries_w, rg[:, lanes])
        carry = jnp.where(start_last < 0.0, jnp.exp(final_cum), 0.0)
        carry_rows.append(jnp.broadcast_to(carry, (8, DH)))
    which = lax.broadcasted_iota(jnp.int32, (8, DH), 0)
    carries = jnp.zeros((8, DH), F32)
    for h in range(PER_GROUP):
        carries = jnp.where(which == h, carry_rows[h], carries)
    own_f[PER_GROUP * DH :, :] = carries
    own_b[PER_GROUP * DH :, :] = carries

    for copy in head_copies:
        copy.wait_recv()
    up, down = (ctx_at(1), g), (ctx_at(-1), g)
    far_up, far_down = (ctx_at(3), g), (ctx_at(-3), g)

    def transfer(sems, n, src, dst, device, sends, receives):
        return send(src, dst, sems[0].at[n], sems[1].at[n], device), sends, receives

    kv_sems, st_sems, gr_sems = (kv_s, kv_r), (st_s, st_r), (gr_s, gr_r)
    over = (ctx_at(4), g)
    inner, outer = (c >= 1) & (x > 0), x == 0
    upper, lower = pl.ds(0, TILE), pl.ds(TILE, TILE)
    kv_copies = [
        transfer(kv_sems, 0, kvb.at[0, 0], kvb.at[1, 0], up, has(1) & (x < 3), inner),
        transfer(kv_sems, 1, kvb.at[0, 1], kvb.at[3, 1], far_up, has(3), has(-3)),
        transfer(kv_sems, 2, kvb.at[0, 1], kvb.at[1, 1], up, has(1) & (x < 3), inner),
        transfer(kv_sems, 3, kvb.at[0, 0], kvb.at[3, 0], far_up, has(3), has(-3)),
        transfer(kv_sems, 4, kvb.at[1, 0, upper], kvb.at[2, 0, upper], up, has(1) & inner, has(-2)),
        transfer(
            kv_sems, 5, kvb.at[3, 1], kvb.at[2, 1], down, has(-3), (c >= 2) & (c < n_ctx - 1)
        ),
        transfer(kv_sems, 6, kvb.at[1, 1], kvb.at[2, 1], up, c == n_ctx - 2, c == n_ctx - 1),
        transfer(
            kv_sems, 7, kvb.at[0, 0, upper], kv_thru.at[0, upper], far_down,
            (x == 3) & has(1), outer & has(4),
        ),
        transfer(kv_sems, 8, kvb.at[0, 1], kv_thru.at[1], far_down, (x == 3) & has(1), outer & has(4)),
        transfer(
            kv_sems, 9, kv_thru.at[0, upper], kvb.at[1, 0, upper], over,
            outer & has(4), outer & has(-4),
        ),
        transfer(kv_sems, 10, kv_thru.at[1], kvb.at[1, 1], over, outer & has(4), outer & has(-4)),
        transfer(
            kv_sems, 4, kvb.at[1, 0, upper], kvb.at[2, 0, upper], up,
            outer & has(1) & has(-4), has(-2),
        ),
        transfer(kv_sems, 11, kvb.at[1, 0, lower], kvb.at[2, 0, lower], up, has(1) & inner, has(-2)),
        transfer(
            kv_sems, 12, kvb.at[0, 0, lower], kv_thru.at[0, lower], far_down,
            (x == 3) & has(1), outer & has(4),
        ),
        transfer(
            kv_sems, 13, kv_thru.at[0, lower], kvb.at[1, 0, lower], over,
            outer & has(4), outer & has(-4),
        ),
        transfer(
            kv_sems, 11, kvb.at[1, 0, lower], kvb.at[2, 0, lower], up,
            outer & has(1) & has(-4), has(-2),
        ),
    ]
    state_copies = [
        transfer(st_sems, 0, own_f, got_f.at[0], up, has(1) & (x < 3), has(-1) & (x > 0)),
        transfer(st_sems, 1, own_b, got_b.at[0], down, has(-1), has(1)),
        transfer(st_sems, 2, own_f, got_f.at[2], far_up, has(3) & (x < 3), has(-3) & (x != 2)),
        transfer(st_sems, 3, own_b, got_b.at[2], far_down, has(-3), has(3)),
        transfer(st_sems, 4, got_f.at[0], got_f.at[1], up, has(1) & has(-1), has(-2)),
        transfer(st_sems, 5, got_b.at[0], got_b.at[1], down, has(1) & has(-1), has(2)),
        transfer(st_sems, 6, own_f, thru, far_down, (x == 3) & has(1), (x == 0) & has(4)),
        transfer(st_sems, 7, own_f, thru, down, (x == 3) & has(3), (x == 2) & has(4)),
        transfer(st_sems, 8, thru, got_f.at[0], over, (x == 0) & has(4), (x == 0) & has(-4)),
        transfer(st_sems, 9, thru, got_f.at[2], over, (x == 2) & has(4), (x == 2) & has(-4)),
    ]
    for n in (7, 13, 0, 1, 8, 2, 3):
        start(kv_copies[n])
    ready_round(2)

    for load in loads[4:]:
        load.wait()

    tile_row = lax.broadcasted_iota(jnp.int32, (TILE, TILE), 0)
    tile_col = lax.broadcasted_iota(jnp.int32, (TILE, TILE), 1)
    tile_pos = tile_row.astype(F32)
    causal = tile_row <= tile_col

    def retention_head(h, nothing):
        lanes = pl.ds(pl.multiple_of(h * DH, DH), DH)
        for ti in range(TILES):
            t = slice(ti * TILE, (ti + 1) * TILE)
            rq_t = rq[t, lanes]
            rg_t = rg[t, lanes]
            cum_t_row = cum_row[pl.ds(h, 1), t]
            query_t = jnp.zeros((DH, TILE), F32)
            for si in range(ti + 1):
                s = slice(si * TILE, (si + 1) * TILE)
                rk_s = rk[s, lanes]
                allowed = tile_pos >= start_row[0:1, t] - float(si * TILE)
                if si == ti:
                    allowed = allowed & causal
                gap = jnp.minimum(cum_t_row - cum_col[h, s, 0:1], 0.0)
                within = jnp.where(allowed, jnp.exp(gap) * SCALING, 0.0)
                grad_w = (within * matmul_nt(rv[s, lanes], rg_t)).astype(BF16)
                score_w = (within * matmul_nt(rk_s, rq_t)).astype(BF16)
                query_t = query_t + matmul_tn(rk_s, grad_w)
                key_term = matmul(grad_w, rq_t)
                value_term = matmul(score_w, rg_t)
                if si == ti:
                    kf[h, s, :] = key_term
                    vf[h, s, :] = value_term
                else:
                    kf[h, s, :] = kf[h, s, :] + key_term
                    vf[h, s, :] = vf[h, s, :] + value_term
            qf[h, t, :] = query_t.T

        return nothing

    lax.fori_loop(0, PER_GROUP, retention_head, 0)

    def tile_strips(i):
        strips = []
        for d in range(DOC_BLOCKS):
            first, stop = (0, (i + 1) * TILE) if d == 0 else (0, ROWS)
            if d == DOC_BLOCKS - 1:
                first = i * TILE
            strips += [(d, at) for at in range(first, stop, STRIP)]
        return strips

    def tile_columns(h, i):
        return pl.ds(pl.multiple_of(i * (PER_GROUP * TILE) + h * TILE, TILE), TILE)

    def scores_of_block(block):
        def one_head(h, nothing):
            for i in range(TILES):
                at_tile = h * TILES + i
                cols = tile_columns(h, i)
                query = qs[cols, :]
                upstream = os[cols, :]
                start_t = start_row[0:1, i * TILE : (i + 1) * TILE]
                top = jnp.full((8, TILE), -1e30, F32) if block == 0 else tops[at_tile]
                for n, (d, at_s) in enumerate(tile_strips(i)):
                    if d != block:
                        continue
                    s = slice(at_s, at_s + STRIP)
                    at = slice(n * STRIP, (n + 1) * STRIP)
                    raw = matmul_nt(kvb[d, 0, s, :], query) * EXPONENT_SCALE
                    allowed = strip_pos >= start_t + float(d * ROWS - at_s)
                    if d == 0 and at_s >= i * TILE:
                        allowed = allowed & (strip_row + (at_s - i * TILE) <= strip_col)
                    raw = jnp.where(allowed, raw, -1e30)
                    score[at_tile, at, :] = raw
                    top = jnp.maximum(top, jnp.max(raw.reshape(STRIP // 8, 8, TILE), axis=0))
                    dprob[at_tile, at, :] = matmul_nt(kvb[d, 1, s, :], upstream)
                tops[at_tile] = top
            return nothing

        lax.fori_loop(0, PER_GROUP, one_head, 0)

    strip_row = lax.broadcasted_iota(jnp.int32, (STRIP, TILE), 0)
    strip_col = lax.broadcasted_iota(jnp.int32, (STRIP, TILE), 1)
    strip_pos = strip_row.astype(F32)

    receive(kv_copies[7])
    start(kv_copies[9])
    receive(kv_copies[13])
    start(kv_copies[14])
    receive(kv_copies[0])
    start(kv_copies[4])
    start(kv_copies[12])
    receive(kv_copies[1])
    start(kv_copies[5])
    for n in (6, 7, 1, 0, 3, 2):
        start(state_copies[n])
    scores_of_block(0)
    receive(kv_copies[9])
    start(kv_copies[11])
    receive(kv_copies[8])
    start(kv_copies[10])
    receive(kv_copies[14])
    start(kv_copies[15])
    receive(kv_copies[2])
    start(kv_copies[6])
    receive(kv_copies[3])
    ready_round(3)
    scores_of_block(3)
    receive(kv_copies[10])
    scores_of_block(1)
    for n in (6, 7):
        receive(state_copies[n])
        start(state_copies[n + 2])
    for d in (0, 1, 3):
        kt[d] = kvb[d, 0].astype(F32).T.astype(BF16)
    for n in (4, 12, 5, 6):
        receive(kv_copies[n])
    kt[2] = kvb[2, 0].astype(F32).T.astype(BF16)
    receive(state_copies[1])
    start(state_copies[5])
    scores_of_block(2)
    receive(state_copies[0])
    receive(state_copies[8])
    start(state_copies[4])

    def attention_head(h, nothing):
        for i in range(TILES):
            at_tile = h * TILES + i
            cols = tile_columns(h, i)
            strips = tile_strips(i)
            top = jnp.max(tops[at_tile], axis=0, keepdims=True)
            total = jnp.zeros((8, TILE), F32)
            for n in range(len(strips)):
                at = slice(n * STRIP, (n + 1) * STRIP)
                term = jnp.exp2(score[at_tile, at, :] - top)
                score[at_tile, at, :] = term
                total = total + jnp.sum(term.reshape(STRIP // 8, 8, TILE), axis=0)
            inverse = 1.0 / jnp.sum(total, axis=0, keepdims=True)
            row_dot = jnp.zeros((8, TILE), F32)
            for n, (d, at_s) in enumerate(strips):
                s = slice(at_s, at_s + STRIP)
                at = slice(n * STRIP, (n + 1) * STRIP)
                weights = score[at_tile, at, :] * inverse
                weights_b = weights.astype(BF16)
                prob_t[d, s, cols] = weights_b
                products = weights_b.astype(F32) * dprob[at_tile, at, :]
                row_dot = row_dot + jnp.sum(products.reshape(STRIP // 8, 8, TILE), axis=0)
            row_dot = jnp.sum(row_dot, axis=0, keepdims=True)
            query_t = jnp.zeros((DH, TILE), F32)
            for n, (d, at_s) in enumerate(strips):
                s = slice(at_s, at_s + STRIP)
                at = slice(n * STRIP, (n + 1) * STRIP)
                gaps = dprob[at_tile, at, :] - row_dot
                dscores_b = ((score[at_tile, at, :] * inverse) * gaps).astype(BF16)
                dscore_t[d, s, cols] = dscores_b
            for d in range(DOC_BLOCKS):
                first, stop = (0, (i + 1) * TILE) if d == 0 else (0, ROWS)
                if d == DOC_BLOCKS - 1:
                    first = i * TILE
                query_t = query_t + matmul(kt[d, :, first:stop], dscore_t[d, first:stop, cols])
            gq[i * TILE : (i + 1) * TILE, pl.ds(pl.multiple_of(h * DH, DH), DH)] = (
                query_t.T * SCALING
            ).astype(BF16)

        @pl.when(h == 0)
        def _():
            ready_round(4)

        @pl.when(h == 1)
        def _():
            ready_round(5)

        return nothing

    lax.fori_loop(0, PER_GROUP, attention_head, 0, unroll=True)

    stores = [pltpu.make_async_copy(gq, gq_out, out_sem.at[0])]
    stores[0].start()

    width = PER_GROUP * TILE

    def partial_at(d, j):
        cols = slice(0, TILES * width)
        if d == 0:
            cols = slice(j * width, TILES * width)
        if d == 3:
            cols = slice(0, (j + 1) * width)
        return slice(j * TILE, (j + 1) * TILE), cols

    middle_device = has(1) & has(-1)
    grad_copies = [
        transfer(gr_sems, 0, part.at[1, 0], half.at[0], down, has(-2), middle_device),
        transfer(gr_sems, 1, part.at[1, 1], half.at[1], up, has(-2) & has(1), has(-3)),
        transfer(gr_sems, 2, part.at[1, 1], half.at[2], down, c == n_ctx - 1, c == n_ctx - 2),
        transfer(gr_sems, 3, part.at[2, 0], back.at[1, 0], far_down, has(-3), has(3)),
        transfer(
            gr_sems, 4, part.at[0, 1], back.at[0, 1], down, has(-1) & (x > 0), has(1) & (x < 3)
        ),
        transfer(gr_sems, 5, part.at[2, 1], back.at[1, 1], far_down, has(-3), has(3)),
        transfer(gr_sems, 6, part.at[0, 0], back.at[0, 0], down, has(-1), has(1)),
        transfer(gr_sems, 7, part.at[0, 1], grad_thru, far_up, (x == 0) & has(-4), (x == 3) & has(-4)),
        transfer(
            gr_sems, 8, grad_thru, back.at[0, 1], (ctx_at(-4), g), (x == 3) & has(-4), (x == 3) & has(4)
        ),
    ]

    def key_grad(d, out, at):
        for j in range(TILES):
            s, cols = partial_at(d, j)
            value = matmul(dscore_t[d, s, cols], qs[cols, :]) * SCALING
            out[at + (s,)] = value.astype(out.dtype)

    def value_grad(d, out, at):
        for j in range(TILES):
            s, cols = partial_at(d, j)
            value = matmul(prob_t[d, s, cols], os[cols, :])
            out[at + (s,)] = value.astype(out.dtype)

    key_grad(2, part, (1, 0))
    start(grad_copies[0])
    value_grad(2, part, (1, 1))
    start(grad_copies[1])
    start(grad_copies[2])
    key_grad(3, part, (2, 0))
    start(grad_copies[3])
    value_grad(1, wait_sum, (0,))

    receive(grad_copies[2])

    part[0, 1] = (wait_sum[0] + half[2].astype(F32)).astype(BF16)
    start(grad_copies[4])
    start(grad_copies[7])
    value_grad(3, wait_sum, (1,))
    key_grad(1, wait_sum, (2,))
    key_grad(0, home, (0,))
    value_grad(0, home, (1,))
    ready_round(6)

    for n in (2, 3, 4, 5, 9):
        receive(state_copies[n])
    sums = jnp.zeros((ROWS, DH), F32)
    lane_at = lax.broadcasted_iota(jnp.int32, (ROWS, DH), 1)
    for h in range(PER_GROUP):
        lanes = slice(h * DH, (h + 1) * DH)
        block = slice(h * DH, (h + 1) * DH)
        carry_at = slice(PER_GROUP * DH + h, PER_GROUP * DH + h + 1)

        def chained(got):
            inner = got[1, block, :] + got[1, carry_at, :] * got[2, block, :]
            return (got[0, block, :] + got[0, carry_at, :] * inner).astype(BF16)

        state_b = jnp.where(c > 0, chained(got_f), jnp.zeros((DH, DH), BF16))
        later_b = jnp.where(c < n_ctx - 1, chained(got_b), jnp.zeros((DH, DH), BF16))
        last = last_w[h]
        query_f = qf[h] + first_w[h] * matmul_nt(rg[:, lanes], state_b)
        key_f = kf[h] + last * matmul_nt(rv[:, lanes], later_b)
        value_f = vf[h] + last * matmul(rk[:, lanes], later_b)
        oq[:, lanes] = query_f.astype(BF16)
        ok[:, lanes] = key_f.astype(BF16)
        ov[:, lanes] = value_f.astype(BF16)
        residue = jnp.sum(rq[:, lanes].astype(F32) * query_f, axis=1, keepdims=True) - jnp.sum(
            rk[:, lanes].astype(F32) * key_f, axis=1, keepdims=True
        )
        sums = jnp.where(lane_at == h, residue, sums)
    for n, (held, target) in enumerate(((oq, oq_out), (ok, ok_out), (ov, ov_out))):
        stores.append(pltpu.make_async_copy(held, target, out_sem.at[n + 1]))
        stores[-1].start()
    suffix = triangle_sum(sums.T[0:16], (row_at >= col_at).astype(F32).astype(BF16))
    cum_row[...] = suffix
    tot_x[0] = jnp.broadcast_to(suffix[0:8, 0:1], (8, DH))
    x_copies = [
        send(tot_x.at[0], tot_x.at[k], tx_s.at[k], tx_r.at[k], (x_peer(k), g))
        for k in range(1, X_RING)
    ]
    for copy in x_copies:
        copy.start()

    receive(grad_copies[7])
    start(grad_copies[8])
    receive(grad_copies[1])
    part[2, 1] = (wait_sum[1] + half[1].astype(F32)).astype(BF16)
    start(grad_copies[5])
    receive(grad_copies[0])
    part[0, 0] = (wait_sum[2] + half[0].astype(F32)).astype(BF16)
    start(grad_copies[6])

    for copy in x_copies:
        copy.wait_recv()
    row_total = tot_x[0]
    tail = jnp.zeros((8, DH), F32)
    for k in range(1, X_RING):
        row_total = row_total + tot_x[k]
        tail = tail + jnp.where(lax.rem(x - k + X_RING, X_RING) > x, tot_x[k], 0.0)
    tot_z[0] = row_total
    z_copies = [
        transfer((tz_s, tz_r), k, tot_z.at[0], tot_z.at[k], (z_peer(-k), g), z_has(-k), z_has(k))
        for k in range(1, z_ring)
    ]
    if z_ring > 2:
        pl.when(z >= z_ring - 1)(lambda: pl.semaphore_wait(ready.at[z_ring - 2], 1))
    for copy in z_copies:
        start(copy)

    for n in (3, 4, 5, 6, 8):
        receive(grad_copies[n])
    for m in range(2):
        total = home[m] + back[0, m].astype(F32) + back[1, m].astype(F32)
        final[m] = total.astype(BF16)
    final_copies = []
    for k in range(1, n_head):
        to = head_at(k)
        copy = send(
            final.at[:, pl.ds(pl.multiple_of(to * slot_rows, slot_rows), slot_rows), :],
            landed.at[:, :, pl.ds(pl.multiple_of(g * DH, DH), DH)],
            fin_s.at[k], fin_r.at[k], (c, to),
        )
        copy.start()
        final_copies.append(copy)
    landed[:, :, pl.ds(pl.multiple_of(g * DH, DH), DH)] = final[
        :, pl.ds(pl.multiple_of(g * slot_rows, slot_rows), slot_rows), :
    ]

    for copy in z_copies:
        receive(copy)
    for k in range(1, z_ring):
        tail = tail + jnp.where(z_has(k), tot_z[k], 0.0)
    dg[...] = (cum_row[0:8, :] + tail[:, 0:1])[0:PER_GROUP]

    for copy in final_copies:
        copy.wait_recv()
    for m, target in enumerate((gk, gv)):
        stores.append(pltpu.make_async_copy(landed.at[m], target, out_sem.at[m + 4]))
        stores[-1].start()
    for store in stores:
        store.wait()
    for copy in head_copies + x_copies + final_copies:
        copy.wait_send()
    for copy in kv_copies + state_copies + grad_copies + z_copies:
        sent(copy)


def write_out(*refs):
    count = 7
    sources, targets, held = refs[:count], refs[count : 2 * count], refs[2 * count : 3 * count]
    sem_in, sem_out = refs[3 * count :]
    loads = [pltpu.make_async_copy(sources[n], held[n], sem_in.at[n]) for n in range(count)]
    stores = [pltpu.make_async_copy(held[n], targets[n], sem_out.at[n]) for n in range(count)]
    for load in loads:
        load.start()
    for load, store in zip(loads, stores):
        load.wait()
        store.start()
    for store in stores:
        store.wait()


def on_device(
    cross_query, cross_grad, cache_keys, cache_values, retention_query, retention_key,
    retention_value, retention_grad, log_decay, doc_offsets,
):
    n_ctx = lax.axis_size("ctx")
    n_head = lax.axis_size("head")
    wide = jax.ShapeDtypeStruct(cross_query.shape, BF16)
    cache = jax.ShapeDtypeStruct(cache_keys.shape, BF16)
    vmem = pl.BlockSpec(memory_space=pltpu.VMEM)
    slot_rows, all_heads = cache_keys.shape
    dma = pltpu.SemaphoreType.DMA
    any_space = pl.BlockSpec(memory_space=pl.ANY)
    heads_wide = pltpu.VMEM((PER_GROUP, ROWS, DH), F32)
    results = pl.pallas_call(
        lambda *refs: body(n_ctx, n_head, *refs),
        out_shape=(
            wide, cache, cache, wide, wide, wide, jax.ShapeDtypeStruct(log_decay.shape, F32),
        ),
        in_specs=[any_space] * 2 + [vmem] * 2 + [any_space] * 4 + [vmem] * 2,
        out_specs=(any_space,) * 6 + (vmem,),
        scratch_shapes=[
            *[pltpu.VMEM(cross_query.shape, BF16)] * 8,
            dma((4,)), dma((2 * PER_GROUP * TILES,)), dma((6,)),
            pltpu.VMEM((2, slot_rows, all_heads), BF16),
            pltpu.VMEM((4, 2, ROWS, DH), BF16),
            pltpu.VMEM((2, ROWS, DH), BF16),
            pltpu.VMEM((STATE_ROWS, DH), F32),
            pltpu.VMEM((STATE_ROWS, DH), F32),
            pltpu.VMEM((3, STATE_ROWS, DH), F32),
            pltpu.VMEM((3, STATE_ROWS, DH), F32),
            pltpu.VMEM((STATE_ROWS, DH), F32),
            pltpu.VMEM((3, 2, ROWS, DH), BF16),
            pltpu.VMEM((3, ROWS, DH), BF16),
            pltpu.VMEM((2, 2, ROWS, DH), BF16),
            pltpu.VMEM((ROWS, DH), BF16),
            pltpu.VMEM((2, ROWS, DH), F32),
            pltpu.VMEM((3, ROWS, DH), F32),
            pltpu.VMEM((2, ROWS, DH), BF16),
            pltpu.VMEM((2, slot_rows, all_heads), BF16),
            pltpu.VMEM((X_RING, 8, DH), F32),
            pltpu.VMEM((max(n_ctx // X_RING, 1), 8, DH), F32),
            pltpu.VMEM((PER_GROUP * ROWS, DH), BF16),
            pltpu.VMEM((PER_GROUP * ROWS, DH), BF16),
            pltpu.VMEM((4, DH, ROWS), BF16),
            pltpu.VMEM((PER_GROUP * TILES, 7 * TILE, TILE), F32),
            pltpu.VMEM((PER_GROUP * TILES, 7 * TILE, TILE), F32),
            pltpu.VMEM((PER_GROUP * TILES, 8, TILE), F32),
            pltpu.VMEM((4, ROWS, PER_GROUP * ROWS), BF16),
            pltpu.VMEM((4, ROWS, PER_GROUP * ROWS), BF16),
            pltpu.VMEM((8, ROWS), F32),
            pltpu.VMEM((16, ROWS), F32),
            heads_wide,
            heads_wide,
            heads_wide,
            heads_wide,
            heads_wide,
            heads_wide,
            pltpu.VMEM((16, ROWS), F32),
            dma((8,)), dma((8,)), dma((14,)), dma((14,)), dma((10,)), dma((10,)), dma((9,)), dma((9,)),
            dma((8,)), dma((8,)), dma((4,)), dma((4,)), dma((8,)), dma((8,)),
            pltpu.SemaphoreType.REGULAR((8,)),
        ],
        compiler_params=pltpu.CompilerParams(
            collective_id=0, has_side_effects=True, vmem_limit_bytes=56 * 1024 * 1024
        ),
    )(
        cross_query, cross_grad, cache_keys, cache_values, retention_query, retention_key,
        retention_value, retention_grad, log_decay, doc_offsets.reshape(1, -1),
    )
    return pl.pallas_call(
        write_out,
        out_shape=tuple(jax.ShapeDtypeStruct(r.shape, r.dtype) for r in results),
        in_specs=[any_space] * 7,
        out_specs=(any_space,) * 7,
        scratch_shapes=[pltpu.VMEM(r.shape, r.dtype) for r in results] + [dma((7,)), dma((7,))],
    )(*results)


def solution(mesh):
    wide = P("ctx", "head")
    cache = P(("ctx", "head"), None)
    return jax.shard_map(
        on_device,
        mesh=mesh,
        in_specs=(wide, wide, cache, cache, wide, wide, wide, wide, P("head", "ctx"), P()),
        out_specs=(wide, cache, cache, wide, wide, wide, P("head", "ctx")),
        check_vma=False,
    )
```
